256 devices in a mesh: intra: 16 (over x, y_lo, core), inter: 16 (over y_hi, z).
Axes of the slice: x: 4, y: 4 (y_hi: 2, y_lo: 2; y = y_hi * 2 + y_lo), z: 8, core: 2. Of those that a mesh axis runs over, the one named last changes fastest.
Arguments:
- hidden_one: bfloat16 [32768, 128], P(('intra', 'inter')), may hold values from -14 to 14
- upstream_one: bfloat16 [32768, 12288], P(('intra', 'inter')), may hold values from -0.0076904297 to 0.0076904297
- hidden_two: bfloat16 [32768, 128], P(('intra', 'inter')), may hold values from -14 to 14
- upstream_two: bfloat16 [32768, 12288], P(('intra', 'inter')), may hold values from -0.0076904297 to 0.0076904297
Outputs:
- grad_one: float32 [128, 12288], P('intra', 'inter')
- grad_two: float32 [128, 12288], P('intra', 'inter')
The draws below stay inside these ranges and needn't reach their ends.
All inputs are finite; a program needn't handle non-finite values.
Results may differ from the reference program's by a relative error of at most 0.0003.
Values may be sent and summed in bfloat16 or wider, within the bound.
No kernel may reach another device: no remote copies, remote signals or barrier semaphores. Data moves between devices by JAX's collectives and lax.ppermute only.
A program may use at most 128 MiB of HBM per device.

```python
import jax
import jax.numpy as jnp
import numpy as np
from jax import lax

D = 12288
R = 128
TOK_DEV = 128
TOKENS = 32768
N_INTRA = 16
N_INTER = 16


def power_lookup(exponents):
    return jnp.asarray([1.0, 2.0, 4.0, 8.0, 16.0], jnp.float32)[exponents]


def activations(key, lowest):
    first, second = jax.random.split(key)
    levels = jax.random.randint(first, (TOKENS, R), lowest, 8).astype(jnp.float32)
    feature = power_lookup(jax.random.randint(second, (1, R), 0, 5))
    return (levels * feature / 8.0).astype(jnp.bfloat16)


def gradients(key, centre, spread):
    first, second, third = jax.random.split(key, 3)
    common = jax.random.randint(first, (1, D), -centre, centre + 1)
    noise = jax.random.randint(second, (TOKENS, D), -spread, spread + 1)
    column = power_lookup(jax.random.randint(third, (1, D), 0, 5))
    return ((common + noise).astype(jnp.float32) * column * 2.0 ** (-17)).astype(jnp.bfloat16)


def draw_hidden_one(key, part):
    key = jax.random.fold_in(key, 11)
    return activations(key, -7)


def draw_upstream_one(key, part):
    key = jax.random.fold_in(key, 12)
    return gradients(key, 0, 63)


def draw_hidden_two(key, part):
    key = jax.random.fold_in(key, 13)
    return activations(key, -7)


def draw_upstream_two(key, part):
    key = jax.random.fold_in(key, 14)
    return gradients(key, 0, 63)


def setup_inputs(seed: int = 0) -> dict:
    key_of = jax.random.split(jax.random.key(seed), 5)
    return {
        "hidden_one": draw_hidden_one(jax.random.fold_in(key_of[4], 71), 0),
        "upstream_one": draw_upstream_one(jax.random.fold_in(key_of[4], 71), 0),
        "hidden_two": draw_hidden_two(jax.random.fold_in(key_of[4], 71), 0),
        "upstream_two": draw_upstream_two(jax.random.fold_in(key_of[4], 71), 0),
    }


POWERS = 2.0 ** np.arange(-40, 31)

def quantize(values):
    extent = values.shape
    blocks = values.reshape(extent[:-1] + (extent[-1] // 128, 128))
    largest = lax.optimization_barrier(jnp.max(jnp.abs(blocks), axis=-1))[..., None]
    powers_table = jnp.asarray(POWERS, jnp.float32)
    inverse_table = jnp.asarray(1.0 / POWERS, jnp.float32)
    covers = largest <= 64.0 * powers_table
    block_steps = lax.optimization_barrier(jnp.min(jnp.where(covers, powers_table, jnp.float32(2.0 ** 31)), axis=-1))
    inverse_steps = lax.optimization_barrier(jnp.max(jnp.where(covers, inverse_table, jnp.float32(0.0)), axis=-1))
    scaled = blocks * inverse_steps[..., None]
    floored = jnp.floor(scaled)
    block_codes = floored + jnp.where(scaled - floored >= 0.5, jnp.float32(1.0), jnp.float32(0.0))
    return (block_codes.astype(jnp.bfloat16).reshape(extent), block_steps)

def restore(packed, scales):
    extent = packed.shape
    blocks = packed.reshape(extent[:-1] + (scales.shape[-1], 128)).astype(jnp.float32)
    return (blocks * scales[..., None]).reshape(extent)

def layer_grad(hidden, upstream):
    hidden_blocks = hidden.reshape(N_INTRA, N_INTER, TOK_DEV, R)
    upstream_blocks = upstream.reshape(N_INTRA, N_INTER, TOK_DEV, D)

    def node_total(total, member):

        def add_source(partial_value, source):
            term = jnp.dot(hidden_blocks[source, member].T, upstream_blocks[source, member], preferred_element_type=jnp.float32)
            packed, scales = quantize(term)
            return (partial_value + restore(packed, scales), None)
        partial_value, unused = lax.scan(add_source, jnp.zeros((R, D), jnp.float32), jnp.arange(N_INTRA, dtype=jnp.int32))
        packed, scales = quantize(partial_value)
        return (total + restore(packed, scales), None)
    total, unused = lax.scan(node_total, jnp.zeros((R, D), jnp.float32), jnp.arange(N_INTER, dtype=jnp.int32))
    return total

def reference(hidden_one, upstream_one, hidden_two, upstream_two):
    return (layer_grad(hidden_one, upstream_one), layer_grad(hidden_two, upstream_two))
```

```python
import functools

import jax
import jax.numpy as jnp
from jax import lax
from jax.experimental import pallas as pl
from jax.experimental.pallas import tpu as pltpu
from jax.sharding import PartitionSpec as P

BLOCK = 128
CHUNK_BLOCKS = 8
LOWEST = 2.0**-34


def round_to_step(values):
    largest = jnp.maximum(jnp.max(jnp.abs(values), axis=-1, keepdims=True), LOWEST)
    raised = largest * 2.0**24
    power = (raised + largest) - raised
    power = jnp.where(power == 0.0, largest, power)
    step = power * 2.0**-6
    half = power * 2.0**-7
    shift = power * (1.5 * 2.0**17)
    nearest = (values + shift) - shift
    return nearest + jnp.where(values - nearest >= half, step, 0.0)


def grad_kernel(groups, hidden_ref, upstream_ref, out_ref):
    hidden = hidden_ref[...]
    share = hidden.shape[1] // groups
    grad = lax.dot_general(
        hidden, upstream_ref[...], (((0,), (0,)), ((), ())), preferred_element_type=jnp.float32
    )
    blocks = grad.shape[1] // BLOCK
    for pair in range(blocks // 2):
        left = round_to_step(grad[:, (2 * pair) * BLOCK : (2 * pair + 1) * BLOCK])
        right = round_to_step(grad[:, (2 * pair + 1) * BLOCK : (2 * pair + 2) * BLOCK])
        rows = left.shape[0]
        both = jnp.concatenate(
            [left.reshape(groups, share, BLOCK), right.reshape(groups, share, BLOCK)], axis=1
        )
        out_ref[:, pair * 2 * share : (pair + 1) * 2 * share, :] = both.astype(jnp.bfloat16)


def local_blocks(hidden, upstream, groups):
    tokens, rows = hidden.shape
    columns = upstream.shape[1]
    share = rows // groups
    blocks = columns // BLOCK
    chunk = CHUNK_BLOCKS
    return pl.pallas_call(
        functools.partial(grad_kernel, groups),
        grid=(blocks // chunk,),
        in_specs=[
            pl.BlockSpec((tokens, rows), lambda c: (0, 0)),
            pl.BlockSpec((tokens, chunk * BLOCK), lambda c: (0, c)),
        ],
        out_specs=pl.BlockSpec((groups, chunk * share, BLOCK), lambda c: (0, c, 0)),
        out_shape=jax.ShapeDtypeStruct((groups, blocks * share, BLOCK), jnp.bfloat16),
        compiler_params=pltpu.CompilerParams(vmem_limit_bytes=32 * 2**20),
        cost_estimate=pl.CostEstimate(
            flops=2 * tokens * rows * columns,
            bytes_accessed=4 * tokens * columns,
            transcendentals=0,
        ),
    )(hidden, upstream)


def node_kernel(pieces_ref, out_ref):
    total = pieces_ref[0].astype(jnp.float32)
    for source in range(1, pieces_ref.shape[0]):
        total = total + pieces_ref[source].astype(jnp.float32)
    out_ref[...] = round_to_step(total).astype(jnp.bfloat16)


def node_blocks(pieces):
    groups, rows, _ = pieces.shape
    tile = rows // 6
    return pl.pallas_call(
        node_kernel,
        grid=(6,),
        in_specs=[pl.BlockSpec((groups, tile, BLOCK), lambda c: (0, c, 0))],
        out_specs=pl.BlockSpec((tile, BLOCK), lambda c: (c, 0)),
        out_shape=jax.ShapeDtypeStruct((rows, BLOCK), jnp.bfloat16),
        compiler_params=pltpu.CompilerParams(vmem_limit_bytes=32 * 2**20),
        cost_estimate=pl.CostEstimate(
            flops=groups * rows * BLOCK,
            bytes_accessed=2 * groups * rows * BLOCK,
            transcendentals=0,
        ),
    )(pieces)


def final_kernel(pieces_ref, out_ref):
    total = pieces_ref[0].astype(jnp.float32)
    for source in range(1, pieces_ref.shape[0]):
        total = total + pieces_ref[source].astype(jnp.float32)
    share = out_ref.shape[0]
    for block in range(out_ref.shape[1] // BLOCK):
        out_ref[:, block * BLOCK : (block + 1) * BLOCK] = total[block * share : (block + 1) * share]


def final_sum(pieces, share):
    owners, rows, _ = pieces.shape
    return pl.pallas_call(
        final_kernel,
        out_shape=jax.ShapeDtypeStruct((share, rows // share * BLOCK), jnp.float32),
    )(pieces)


def body(hidden_one, upstream_one, hidden_two, upstream_two):
    groups = lax.axis_size("intra")
    owners = lax.axis_size("inter")
    share = hidden_one.shape[1] // groups

    def reduce_layer(hidden, upstream):
        blocks = local_blocks(hidden, upstream, groups)
        pieces = lax.all_to_all(blocks, "intra", split_axis=0, concat_axis=0, tiled=True)
        node = node_blocks(pieces)
        node = node.reshape(owners, node.shape[0] // owners, BLOCK)
        pieces = lax.all_to_all(node, "inter", split_axis=0, concat_axis=0, tiled=True)
        return final_sum(pieces, share)

    first = reduce_layer(hidden_one, upstream_one)
    second = reduce_layer(hidden_two, upstream_two)
    return (first, second)


def solution(mesh):
    return jax.shard_map(
        body,
        mesh=mesh,
        in_specs=(
            P(("intra", "inter"), None),
            P(("intra", "inter"), None),
            P(("intra", "inter"), None),
            P(("intra", "inter"), None),
        ),
        out_specs=(P("intra", "inter"), P("intra", "inter")),
        check_vma=False,
    )
```

```python
import functools

import jax
import jax.numpy as jnp
from jax import lax
from jax.experimental import pallas as pl
from jax.experimental.pallas import tpu as pltpu
from jax.sharding import PartitionSpec as P

BLOCK = 128
SHARE = 8
LOWEST = 2.0**-34
X, Y, CORES = 4, 2, 2
OWNERS = 16
FIRST = 5
STEPS = OWNERS // 2
LAYER = 6
SMALL = pl.CostEstimate(flops=1, bytes_accessed=1, transcendentals=0)
PARAMS = pltpu.CompilerParams(vmem_limit_bytes=32 * 2**20)


def node_pairs(move):
    pairs = []
    for x in range(X):
        for y in range(Y):
            for core in range(CORES):
                to_x, to_y, to_core = move(x, y, core)
                pairs.append(((x * Y + y) * CORES + core, (to_x % X * Y + to_y) * CORES + to_core))
    return pairs


TO_CORE = node_pairs(lambda x, y, core: (x, y, 1 - core))
TO_Y = node_pairs(lambda x, y, core: (x, 1 - y, core))
TO_RIGHT = node_pairs(lambda x, y, core: (x + 1, y, core))
TO_LEFT = node_pairs(lambda x, y, core: (x - 1, y, core))


def send(array, pairs):
    return lax.ppermute(array, "intra", pairs)


def round_to_step(values):
    largest = jnp.maximum(jnp.max(jnp.abs(values), axis=-1, keepdims=True), LOWEST)
    raised = largest * 2.0**24
    power = (raised + largest) - raised
    power = jnp.where(power == 0.0, largest, power)
    step = power * 2.0**-6
    half = power * 2.0**-7
    shift = power * (1.5 * 2.0**17)
    nearest = (values + shift) - shift
    return nearest + jnp.where(values - nearest >= half, step, 0.0)


def ordered(hidden, me, along_y_first):
    rows = hidden.shape[1]
    place = lax.broadcasted_iota(jnp.int32, (rows, rows), 0)
    row = lax.broadcasted_iota(jnp.int32, (rows, rows), 1)
    core = place // 64
    if along_y_first:
        y, x = place // 32 % 2, place // 8 % 4
    else:
        x, y = place // 16 % 4, place // 8 % 2
    x = (x + me // 4) % X
    y = (y + me // 2) % Y
    core = (core + me) % CORES
    source = ((x * Y + y) * CORES + core) * SHARE + place % SHARE
    chosen = jnp.where(row == source, 1.0, 0.0).astype(jnp.bfloat16)
    return lax.dot_general(
        chosen, hidden, (((1,), (1,)), ((), ())), preferred_element_type=jnp.float32
    ).astype(jnp.bfloat16)


def gradient_kernel(shares, first, me_ref, *refs):
    count = len(shares)
    sources, (keep_ref, send_ref), places = refs[: 2 * count], refs[2 * count : 2 * count + 2], refs[2 * count + 2 : -1]
    arrived = refs[-1]

    def copies(step):
        found = []
        for layer, share in enumerate(shares):
            upstream, place = sources[2 * layer + 1], places[2 * layer + 1]
            width = len(share) * BLOCK
            for owner in range(2):
                start = (step * 2 + owner) * LAYER * BLOCK + share[0] * BLOCK
                found.append(
                    pltpu.make_async_copy(
                        upstream.at[:, pl.ds(pl.multiple_of(start, BLOCK), width)],
                        place.at[step, owner],
                        arrived.at[layer, step, owner],
                    )
                )
        return found

    heads = [
        pltpu.make_async_copy(sources[2 * layer], places[2 * layer], arrived.at[layer, STEPS, 0])
        for layer in range(count)
    ]
    for copy in heads:
        copy.start()
    for step in range(STEPS):
        for copy in copies(step):
            copy.start()
    for copy in heads:
        copy.wait()
    left = [ordered(places[2 * layer][...], me_ref[0], first) for layer in range(count)]
    rows = 2 * SHARE * sum(len(share) for share in shares)

    def one_step(step, carry):
        for copy in copies(step):
            copy.wait()
        blocks = []
        for owner in range(2):
            for layer, share in enumerate(shares):
                for block in range(len(share)):
                    blocks.append((layer, owner, block))
        for pair in range(len(blocks) // 2):
            both = []
            for layer, owner, block in blocks[2 * pair : 2 * pair + 2]:
                upstream = places[2 * layer + 1][step, owner, :, block * BLOCK : (block + 1) * BLOCK]
                grad = jnp.dot(left[layer], upstream, preferred_element_type=jnp.float32)
                both.append(round_to_step(grad).reshape(16, SHARE, BLOCK))
            both = jnp.concatenate(both, axis=1).astype(jnp.bfloat16)
            at = pl.ds(pl.multiple_of(step * rows + pair * 2 * SHARE, 2 * SHARE), 2 * SHARE)
            keep_ref[:, at, :] = both[:8]
            send_ref[:, at, :] = both[8:]
        return carry

    lax.fori_loop(0, STEPS, one_step, 0)


def gradients(me, layers, shares, first):
    tokens, rows = layers[0][0].shape
    out = jax.ShapeDtypeStruct((8, OWNERS * sum(len(share) for share in shares) * SHARE, BLOCK), jnp.bfloat16)
    places = []
    for share in shares:
        places.append(pltpu.VMEM((tokens, rows), jnp.bfloat16))
        places.append(pltpu.VMEM((STEPS, 2, tokens, len(share) * BLOCK), jnp.bfloat16))
    return pl.pallas_call(
        functools.partial(gradient_kernel, shares, first),
        in_specs=[pl.BlockSpec(memory_space=pltpu.SMEM)]
        + [pl.BlockSpec(memory_space=pltpu.HBM)] * (2 * len(layers)),
        out_specs=[pl.BlockSpec(memory_space=pltpu.VMEM)] * 2,
        out_shape=[out, out],
        scratch_shapes=places + [pltpu.SemaphoreType.DMA((len(layers), STEPS + 1, 2))],
        compiler_params=pltpu.CompilerParams(vmem_limit_bytes=(55 if len(layers) > 1 else 51) * 2**20),
        cost_estimate=SMALL,
    )(me, *[array for layer in layers for array in layer])


def tiled_call(kernel, steps, ins, outs, after=()):
    if after:
        inner = kernel

        def kernel(*refs):
            inner(*refs[: len(ins)], *refs[len(ins) + len(after) :])

    def spec(shape):
        tile = shape[-2] // steps
        lead = len(shape) - 2
        return pl.BlockSpec(shape[:-2] + (tile, BLOCK), lambda c: (0,) * lead + (c, 0))

    shapes = [jax.ShapeDtypeStruct(tuple(lead) + (rows, BLOCK), dtype) for lead, rows, dtype in outs]
    return pl.pallas_call(
        kernel,
        grid=(steps,),
        in_specs=[spec(a.shape) for a in ins] + [pl.BlockSpec(memory_space=pl.ANY)] * len(after),
        out_specs=[spec(s.shape) for s in shapes],
        out_shape=shapes,
        compiler_params=PARAMS,
        cost_estimate=SMALL,
    )(*ins, *after)


def up(ref, *index):
    return ref[index].astype(jnp.float32) if index else ref[...].astype(jnp.float32)


def pair_kernel(keep_ref, got_ref, stay_ref, go_ref):
    for part in range(4):
        stay_ref[part] = up(keep_ref, part) + up(got_ref, part)
        go_ref[part] = up(keep_ref, part + 4) + up(got_ref, part + 4)


def add_kernel(keep_ref, got_ref, own_ref, right_ref, left_ref, right_later_ref, left_later_ref):
    def total(x, half):
        return up(keep_ref, x, half) + up(got_ref, x, half)

    own_ref[0], own_ref[1] = total(0, 0), total(0, 1)
    right_ref[0], right_ref[1] = total(2, 0), total(1, 1)
    left_ref[0], left_ref[1] = total(2, 1), total(3, 0)
    right_later_ref[...] = total(1, 0)
    left_later_ref[...] = total(3, 1)


def fold_kernel(right_ref, left_ref, from_left_ref, from_right_ref, to_right_ref, to_left_ref):
    to_right_ref[...] = right_ref[...] + from_left_ref[0]
    to_left_ref[...] = left_ref[...] + from_right_ref[0]


def halves(own_ref, from_left_ref, from_right_ref, later_left_ref, later_right_ref):
    first = own_ref[0] + later_left_ref[...] + from_right_ref[1]
    second = own_ref[1] + from_left_ref[1] + later_right_ref[...]
    return first, second


def node_pairs_kernel(own_ref, from_left_ref, from_right_ref, later_left_ref, later_right_ref, stay_ref, go_ref):
    stay_ref[...], go_ref[...] = halves(own_ref, from_left_ref, from_right_ref, later_left_ref, later_right_ref)


def nodes_kernel(own_ref, from_left_ref, from_right_ref, later_left_ref, later_right_ref, stay_ref, got_ref, out_ref):
    first = halves(own_ref, from_left_ref, from_right_ref, later_left_ref, later_right_ref)
    first = jnp.concatenate([round_to_step(half).astype(jnp.bfloat16) for half in first], axis=0)
    second = round_to_step(stay_ref[...] + got_ref[...]).astype(jnp.bfloat16)
    rows = first.shape[0] // OWNERS
    more = second.shape[0] // OWNERS
    for owner in range(OWNERS):
        out_ref[owner, :rows] = first[owner * rows : (owner + 1) * rows]
        out_ref[owner, rows:] = second[owner * more : (owner + 1) * more]


def final_kernel(pieces_ref, one_ref, two_ref):
    total = up(pieces_ref, 0)
    for source in range(1, OWNERS):
        total = total + up(pieces_ref, source)
    for block in range(LAYER):
        columns = slice(block * BLOCK, (block + 1) * BLOCK)
        one_ref[:, columns] = total[block * SHARE : (block + 1) * SHARE]
        two_ref[:, columns] = total[(LAYER + block) * SHARE : (LAYER + block + 1) * SHARE]


def along_x(keep, got, after):
    rows = keep.shape[2]
    f32 = jnp.float32
    own, right, left, right_later, left_later = tiled_call(
        add_kernel, 4, (keep, got), [((2,), rows, f32)] * 3 + [((), rows, f32)] * 2, after[0]
    )
    from_left, from_right = send(right, TO_RIGHT), send(left, TO_LEFT)
    right, left = tiled_call(
        fold_kernel, 1, (right_later, left_later, from_left, from_right), [((), rows, f32)] * 2, after[1]
    )
    return own, from_left, from_right, send(right, TO_RIGHT), send(left, TO_LEFT)


def body(hidden_one, upstream_one, hidden_two, upstream_two):
    f32, bf16 = jnp.float32, jnp.bfloat16
    me = lax.axis_index("intra").astype(jnp.int32).reshape(1)
    one, two = (hidden_one, upstream_one), (hidden_two, upstream_two)
    early, late, every = tuple(range(FIRST)), tuple(range(FIRST, LAYER)), tuple(range(LAYER))

    keep_b, go_b = gradients(me, (one, two), (late, every), False)
    core_b = send(go_b, TO_CORE)
    keep_a, go_a = gradients(me, (one,), (early,), True)
    core_a = send(go_a, TO_CORE)

    more, many = keep_b.shape[1], keep_a.shape[1]
    b = along_x(keep_b.reshape(4, 2, more, BLOCK), core_b.reshape(4, 2, more, BLOCK), ((), ()))
    stay_a, go_a = tiled_call(pair_kernel, 4, (keep_a, core_a), [((4,), many, f32)] * 2, (b[0],))
    y_a = send(go_a, TO_Y)

    stay_b, go_b = tiled_call(node_pairs_kernel, 2, b, [((), more, f32)] * 2)
    y_b = send(go_b, TO_Y)
    a = along_x(
        stay_a.reshape(4, 2, many // 2, BLOCK), y_a.reshape(4, 2, many // 2, BLOCK), ((b[3], b[4]), (go_b,))
    )

    node = pl.pallas_call(
        nodes_kernel,
        out_shape=jax.ShapeDtypeStruct((OWNERS, 2 * LAYER * SHARE, BLOCK), bf16),
        compiler_params=PARAMS,
    )(*a, stay_b, y_b)
    pieces = lax.all_to_all(node, "inter", split_axis=0, concat_axis=0, tiled=True)
    out = jax.ShapeDtypeStruct((SHARE, LAYER * BLOCK), f32)
    return pl.pallas_call(final_kernel, out_shape=(out, out))(pieces)


def solution(mesh):
    return jax.shard_map(
        body,
        mesh=mesh,
        in_specs=(
            P(("intra", "inter"), None),
            P(("intra", "inter"), None),
            P(("intra", "inter"), None),
            P(("intra", "inter"), None),
        ),
        out_specs=(P("intra", "inter"), P("intra", "inter")),
        check_vma=False,
    )
```

```python
import functools

import jax
import jax.numpy as jnp
from jax import lax
from jax.experimental import pallas as pl
from jax.experimental.pallas import tpu as pltpu
from jax.sharding import PartitionSpec as P

BLOCK = 128
SHARE = 8
LOWEST = 2.0**-34
X, Y, CORES = 4, 2, 2
OWNERS = 16
STEPS = OWNERS // 2
LAYER = 6
FIRST = 4
ROOM = (50, 46, 46)
SMALL = pl.CostEstimate(flops=1, bytes_accessed=1, transcendentals=0)
PARAMS = pltpu.CompilerParams(vmem_limit_bytes=32 * 2**20)


def node_pairs(move):
    pairs = []
    for x in range(X):
        for y in range(Y):
            for core in range(CORES):
                to_x, to_y, to_core = move(x, y, core)
                pairs.append(((x * Y + y) * CORES + core, (to_x % X * Y + to_y) * CORES + to_core))
    return pairs


TO_CORE = node_pairs(lambda x, y, core: (x, y, 1 - core))
TO_Y = node_pairs(lambda x, y, core: (x, 1 - y, core))
TO_FIRST = node_pairs(lambda x, y, core: (x + 1 - 2 * (x % 2), y, core))
TO_SECOND = node_pairs(lambda x, y, core: (x - 1 + 2 * (x % 2), y, core))


def send(array, pairs):
    return lax.ppermute(array, "intra", pairs)


def round_to_step(values):
    largest = jnp.maximum(jnp.max(jnp.abs(values), axis=-1, keepdims=True), LOWEST)
    gap = largest - largest * (1.0 - 2.0**-24)
    step = gap * 2.0**18
    half = gap * 2.0**17
    shift = gap * (1.5 * 2.0**41)
    nearest = (values + shift) - shift
    return nearest + jnp.where(values - nearest >= half, step, 0.0)


def ordered(hidden, me, along_y_first):
    rows = hidden.shape[1]
    place = lax.broadcasted_iota(jnp.int32, (rows, rows), 0)
    row = lax.broadcasted_iota(jnp.int32, (rows, rows), 1)
    core = place // 64
    if along_y_first:
        y, x = place // 32 % 2, place // 8 % 4
    else:
        x, y = place // 16 % 4, place // 8 % 2
    own_x = me // 4
    x = (own_x + x * (1 - 2 * (own_x % 2)) + X) % X
    y = (y + me // 2) % Y
    core = (core + me) % CORES
    source = ((x * Y + y) * CORES + core) * SHARE + place % SHARE
    chosen = jnp.where(row == source, 1.0, 0.0).astype(jnp.bfloat16)
    return lax.dot_general(
        chosen, hidden, (((1,), (1,)), ((), ())), preferred_element_type=jnp.float32
    ).astype(jnp.bfloat16)


def gradient_kernel(share, along_y_first, waits, me_ref, hidden_ref, upstream_ref, *refs):
    if waits:
        refs = refs[waits:]
    keep_ref, send_ref, place, arrived = refs
    rows = 2 * SHARE * len(share)
    width = len(share) * BLOCK

    def copies(step):
        found = []
        for owner in range(2):
            start = (step * 2 + owner) * LAYER * BLOCK + share[0] * BLOCK
            source = upstream_ref.at[:, pl.ds(pl.multiple_of(start, BLOCK), width)]
            found.append(pltpu.make_async_copy(source, place.at[step, owner], arrived.at[step, owner]))
        return found

    for step in range(STEPS):
        for copy in copies(step):
            copy.start()
    left = ordered(hidden_ref[...], me_ref[0], along_y_first)

    def one_step(step, carry):
        for copy in copies(step):
            copy.wait()
        blocks = [(owner, block) for owner in range(2) for block in range(len(share))]
        for pair in range(len(share)):
            both = []
            for owner, block in blocks[2 * pair : 2 * pair + 2]:
                upstream = place[step, owner, :, block * BLOCK : (block + 1) * BLOCK]
                grad = jnp.dot(left, upstream, preferred_element_type=jnp.float32)
                both.append(round_to_step(grad).reshape(16, SHARE, BLOCK))
            both = jnp.concatenate(both, axis=1).astype(jnp.bfloat16)
            at = pl.ds(pl.multiple_of(step * rows + pair * 2 * SHARE, 2 * SHARE), 2 * SHARE)
            keep_ref[:, at, :] = both[:8]
            send_ref[:, at, :] = both[8:]
        return carry

    lax.fori_loop(0, STEPS, one_step, 0)


def gradients(me, hidden, upstream, share, along_y_first, room, after=()):
    tokens = upstream.shape[0]
    out = jax.ShapeDtypeStruct((8, OWNERS * len(share) * SHARE, BLOCK), jnp.bfloat16)
    return pl.pallas_call(
        functools.partial(gradient_kernel, share, along_y_first, len(after)),
        in_specs=[
            pl.BlockSpec(memory_space=pltpu.SMEM),
            pl.BlockSpec(memory_space=pltpu.VMEM),
            pl.BlockSpec(memory_space=pltpu.HBM),
        ]
        + [pl.BlockSpec(memory_space=pl.ANY)] * len(after),
        out_specs=[pl.BlockSpec(memory_space=pltpu.VMEM)] * 2,
        out_shape=[out, out],
        scratch_shapes=[
            pltpu.VMEM((STEPS, 2, tokens, len(share) * BLOCK), jnp.bfloat16),
            pltpu.SemaphoreType.DMA((STEPS, 2)),
        ],
        compiler_params=pltpu.CompilerParams(vmem_limit_bytes=room * 2**20),
        cost_estimate=SMALL,
    )(me, hidden, upstream, *after)


def tiled_call(kernel, steps, ins, outs, after=()):
    if after:
        inner = kernel

        def kernel(*refs):
            inner(*refs[: len(ins)], *refs[len(ins) + len(after) :])

    def spec(shape):
        tile = shape[-2] // steps
        lead = len(shape) - 2
        return pl.BlockSpec(shape[:-2] + (tile, BLOCK), lambda c: (0,) * lead + (c, 0))

    shapes = [jax.ShapeDtypeStruct(tuple(lead) + (rows, BLOCK), dtype) for lead, rows, dtype in outs]
    return pl.pallas_call(
        kernel,
        grid=(steps,),
        in_specs=[spec(a.shape) for a in ins] + [pl.BlockSpec(memory_space=pl.ANY)] * len(after),
        out_specs=[spec(s.shape) for s in shapes],
        out_shape=shapes,
        compiler_params=PARAMS,
        cost_estimate=SMALL,
    )(*ins, *after)


def up(ref, *index):
    return ref[index].astype(jnp.float32) if index else ref[...].astype(jnp.float32)


def pair_kernel(keep_ref, got_ref, stay_ref, go_ref):
    for part in range(4):
        stay_ref[part] = up(keep_ref, part) + up(got_ref, part)
        go_ref[part] = up(keep_ref, part + 4) + up(got_ref, part + 4)


def add_kernel(keep_ref, got_ref, own_ref, first_ref, second_ref, first_later_ref, second_later_ref):
    def total(x, half):
        return up(keep_ref, x, half) + up(got_ref, x, half)

    own_ref[0], own_ref[1] = total(0, 0), total(0, 1)
    first_ref[0], first_ref[1] = total(2, 0), total(1, 0)
    second_ref[0], second_ref[1] = total(2, 1), total(3, 1)
    first_later_ref[...] = total(1, 1)
    second_later_ref[...] = total(3, 0)


def fold_kernel(first_ref, second_ref, from_first_ref, from_second_ref, to_first_ref, to_second_ref):
    to_first_ref[...] = first_ref[...] + from_second_ref[0]
    to_second_ref[...] = second_ref[...] + from_first_ref[0]


def halves(own_ref, from_first_ref, from_second_ref, later_first_ref, later_second_ref):
    first = own_ref[0] + from_first_ref[1] + later_second_ref[...]
    second = own_ref[1] + from_second_ref[1] + later_first_ref[...]
    return first, second


def node_pairs_kernel(own_ref, from_first_ref, from_second_ref, later_first_ref, later_second_ref, stay_ref, go_ref):
    stay_ref[...], go_ref[...] = halves(own_ref, from_first_ref, from_second_ref, later_first_ref, later_second_ref)


def nodes_kernel(*refs):
    out_ref = refs[-1]
    parts = []
    for share in (refs[:5], refs[5:10]):
        parts.append(jnp.concatenate([round_to_step(half).astype(jnp.bfloat16) for half in halves(*share)], axis=0))
    stay_ref, got_ref = refs[10:12]
    parts.append(round_to_step(stay_ref[...] + got_ref[...]).astype(jnp.bfloat16))
    at = 0
    for part in parts:
        rows = part.shape[0] // OWNERS
        for owner in range(OWNERS):
            out_ref[owner, at : at + rows] = part[owner * rows : (owner + 1) * rows]
        at += rows


def final_kernel(pieces_ref, one_ref, two_ref):
    total = up(pieces_ref, 0)
    for source in range(1, OWNERS):
        total = total + up(pieces_ref, source)
    for block in range(LAYER):
        columns = slice(block * BLOCK, (block + 1) * BLOCK)
        one_ref[:, columns] = total[block * SHARE : (block + 1) * SHARE]
        two_ref[:, columns] = total[(LAYER + block) * SHARE : (LAYER + block + 1) * SHARE]


def start_x(keep, got, after=()):
    rows = keep.shape[2]
    f32 = jnp.float32
    own, first, second, first_later, second_later = tiled_call(
        add_kernel, 4, (keep, got), [((2,), rows, f32)] * 3 + [((), rows, f32)] * 2, after
    )
    return own, first_later, second_later, send(first, TO_FIRST), send(second, TO_SECOND)


def end_x(own, first_later, second_later, from_first, from_second, after=()):
    rows = own.shape[1]
    first, second = tiled_call(
        fold_kernel, 1, (first_later, second_later, from_first, from_second), [((), rows, jnp.float32)] * 2, after
    )
    return (own, from_first, from_second, send(first, TO_FIRST), send(second, TO_SECOND)), (first, second)


def body(hidden_one, upstream_one, hidden_two, upstream_two):
    f32, bf16 = jnp.float32, jnp.bfloat16
    me = lax.axis_index("intra").astype(jnp.int32).reshape(1)

    def pair(keep, got, after=()):
        return tiled_call(pair_kernel, 4, (keep, got), [((4,), keep.shape[1], f32)] * 2, after)

    def halved(array, parts):
        rows = array.size // BLOCK // parts // 2
        return array.reshape(parts, 2, rows, BLOCK)

    keep_b, go_b = gradients(me, hidden_two, upstream_two, tuple(range(LAYER)), False, ROOM[0])
    core_b = send(go_b, TO_CORE)
    keep_a, go_a = gradients(me, hidden_one, upstream_one, tuple(range(FIRST)), True, ROOM[1])
    core_a = send(go_a, TO_CORE)
    b = start_x(halved(keep_b, 4), halved(core_b, 4))
    stay_a, go_a = pair(keep_a, core_a, (b[0],))
    y_a = send(go_a, TO_Y)
    keep_c, go_c = gradients(me, hidden_one, upstream_one, tuple(range(FIRST, LAYER)), True, ROOM[2], (stay_a,))
    core_c = send(go_c, TO_CORE)
    stay_c, go_c = pair(keep_c, core_c)
    y_c = send(go_c, TO_Y)

    b, sent_b = end_x(*b, (go_c,))
    a = start_x(halved(stay_a, 4), halved(y_a, 4), sent_b)
    stay_b, go_b = tiled_call(node_pairs_kernel, 2, b, [((), b[0].shape[1], f32)] * 2, (a[0],))
    y_b = send(go_b, TO_Y)
    c = start_x(halved(stay_c, 4), halved(y_c, 4), (go_b,))
    a, sent_a = end_x(*a, (c[0],))
    c, _ = end_x(*c, sent_a)

    node = pl.pallas_call(
        nodes_kernel,
        out_shape=jax.ShapeDtypeStruct((OWNERS, 2 * LAYER * SHARE, BLOCK), bf16),
        compiler_params=PARAMS,
        cost_estimate=SMALL,
    )(*a, *c, stay_b, y_b)
    pieces = lax.all_to_all(node, "inter", split_axis=0, concat_axis=0, tiled=True)
    out = jax.ShapeDtypeStruct((SHARE, LAYER * BLOCK), f32)
    return pl.pallas_call(final_kernel, out_shape=(out, out))(pieces)


def solution(mesh):
    return jax.shard_map(
        body,
        mesh=mesh,
        in_specs=(
            P(("intra", "inter"), None),
            P(("intra", "inter"), None),
            P(("intra", "inter"), None),
            P(("intra", "inter"), None),
        ),
        out_specs=(P("intra", "inter"), P("intra", "inter")),
        check_vma=False,
    )
```

```python
import functools

import jax
import jax.numpy as jnp
from jax import lax
from jax.experimental import pallas as pl
from jax.experimental.pallas import tpu as pltpu
from jax.sharding import PartitionSpec as P

BLOCK = 128
SHARE = 8
LOWEST = 2.0**-34
X, Y, CORES = 4, 2, 2
OWNERS = 16
STEPS = OWNERS // 2
LAYER = 6
FIRST = 4
ROOM = (50, 46, 46)
SMALL = pl.CostEstimate(flops=1, bytes_accessed=1, transcendentals=0)
PARAMS = pltpu.CompilerParams(vmem_limit_bytes=32 * 2**20)


def node_pairs(move):
    pairs = []
    for x in range(X):
        for y in range(Y):
            for core in range(CORES):
                to_x, to_y, to_core = move(x, y, core)
                pairs.append(((x * Y + y) * CORES + core, (to_x % X * Y + to_y) * CORES + to_core))
    return pairs


TO_CORE = node_pairs(lambda x, y, core: (x, y, 1 - core))
TO_Y = node_pairs(lambda x, y, core: (x, 1 - y, core))
TO_FIRST = node_pairs(lambda x, y, core: (x + 1 - 2 * (x % 2), y, core))
TO_FAR = node_pairs(lambda x, y, core: (x + 2, y, core))
TO_SECOND = node_pairs(lambda x, y, core: (x - 1 + 2 * (x % 2), y, core))


def send(array, pairs):
    return lax.ppermute(array, "intra", pairs)


def round_to_step(values):
    largest = jnp.maximum(jnp.max(jnp.abs(values), axis=-1, keepdims=True), LOWEST)
    gap = largest - largest * (1.0 - 2.0**-24)
    step = gap * 2.0**18
    half = gap * 2.0**17
    shift = gap * (1.5 * 2.0**41)
    nearest = (values + shift) - shift
    return nearest + jnp.where(values - nearest >= half, step, 0.0)


def ordered(hidden, me, along_y_first):
    rows = hidden.shape[1]
    place = lax.broadcasted_iota(jnp.int32, (rows, rows), 0)
    row = lax.broadcasted_iota(jnp.int32, (rows, rows), 1)
    core = place // 64
    if along_y_first:
        y, x = place // 32 % 2, place // 8 % 4
    else:
        x, y = place // 16 % 4, place // 8 % 2
    own_x = me // 4
    x = (own_x + x * (1 - 2 * (own_x % 2)) + X) % X
    y = (y + me // 2) % Y
    core = (core + me) % CORES
    source = ((x * Y + y) * CORES + core) * SHARE + place % SHARE
    chosen = jnp.where(row == source, 1.0, 0.0).astype(jnp.bfloat16)
    return lax.dot_general(
        chosen, hidden, (((1,), (1,)), ((), ())), preferred_element_type=jnp.float32
    ).astype(jnp.bfloat16)


def gradient_kernel(share, along_y_first, waits, me_ref, hidden_ref, upstream_ref, *refs):
    if waits:
        refs = refs[waits:]
    keep_ref, send_ref, place, arrived = refs
    rows = 2 * SHARE * len(share)
    width = len(share) * BLOCK

    def copies(step):
        found = []
        for owner in range(2):
            start = (step * 2 + owner) * LAYER * BLOCK + share[0] * BLOCK
            source = upstream_ref.at[:, pl.ds(pl.multiple_of(start, BLOCK), width)]
            found.append(pltpu.make_async_copy(source, place.at[step, owner], arrived.at[step, owner]))
        return found

    for step in range(STEPS):
        for copy in copies(step):
            copy.start()
    left = ordered(hidden_ref[...], me_ref[0], along_y_first)

    def one_step(step, carry):
        for copy in copies(step):
            copy.wait()
        blocks = [(owner, block) for owner in range(2) for block in range(len(share))]
        for pair in range(len(share)):
            both = []
            for owner, block in blocks[2 * pair : 2 * pair + 2]:
                upstream = place[step, owner, :, block * BLOCK : (block + 1) * BLOCK]
                grad = jnp.dot(left, upstream, preferred_element_type=jnp.float32)
                both.append(round_to_step(grad).reshape(16, SHARE, BLOCK))
            both = jnp.concatenate(both, axis=1).astype(jnp.bfloat16)
            at = pl.ds(pl.multiple_of(step * rows + pair * 2 * SHARE, 2 * SHARE), 2 * SHARE)
            keep_ref[:, at, :] = both[:8]
            send_ref[:, at, :] = both[8:]
        return carry

    lax.fori_loop(0, STEPS, one_step, 0)


def gradients(me, hidden, upstream, share, along_y_first, room, after=()):
    tokens = upstream.shape[0]
    out = jax.ShapeDtypeStruct((8, OWNERS * len(share) * SHARE, BLOCK), jnp.bfloat16)
    return pl.pallas_call(
        functools.partial(gradient_kernel, share, along_y_first, len(after)),
        in_specs=[
            pl.BlockSpec(memory_space=pltpu.SMEM),
            pl.BlockSpec(memory_space=pltpu.VMEM),
            pl.BlockSpec(memory_space=pltpu.HBM),
        ]
        + [pl.BlockSpec(memory_space=pl.ANY)] * len(after),
        out_specs=[pl.BlockSpec(memory_space=pltpu.VMEM)] * 2,
        out_shape=[out, out],
        scratch_shapes=[
            pltpu.VMEM((STEPS, 2, tokens, len(share) * BLOCK), jnp.bfloat16),
            pltpu.SemaphoreType.DMA((STEPS, 2)),
        ],
        compiler_params=pltpu.CompilerParams(vmem_limit_bytes=room * 2**20),
        cost_estimate=SMALL,
    )(me, hidden, upstream, *after)


def tiled_call(kernel, steps, ins, outs, after=()):
    shapes = [jax.ShapeDtypeStruct(tuple(lead) + (rows, BLOCK), dtype) for lead, rows, dtype in outs]

    def view(ref, step):
        tile = ref.shape[-2] // steps
        rows = pl.ds(pl.multiple_of(step * tile, tile), tile)
        return ref.at[(slice(None),) * (len(ref.shape) - 2) + (rows, slice(None))]

    def whole(*refs):
        used = refs[: len(ins)] + refs[len(ins) + len(after) :]

        def one_step(step, carry):
            kernel(*[view(ref, step) for ref in used])
            return carry

        lax.fori_loop(0, steps, one_step, 0)

    return pl.pallas_call(
        whole if steps > 1 else lambda *refs: kernel(*refs[: len(ins)], *refs[len(ins) + len(after) :]),
        in_specs=[pl.BlockSpec(memory_space=pltpu.VMEM)] * len(ins)
        + [pl.BlockSpec(memory_space=pl.ANY)] * len(after),
        out_specs=[pl.BlockSpec(memory_space=pltpu.VMEM)] * len(shapes),
        out_shape=shapes,
        compiler_params=PARAMS,
        cost_estimate=SMALL,
    )(*ins, *after)


def up(ref, *index):
    return ref[index].astype(jnp.float32) if index else ref[...].astype(jnp.float32)


def pair_kernel(keep_ref, got_ref, stay_ref, go_ref):
    for part in range(4):
        stay_ref[part] = up(keep_ref, part) + up(got_ref, part)
        go_ref[part] = up(keep_ref, part + 4) + up(got_ref, part + 4)


def add_kernel(keep_ref, got_ref, own_ref, first_ref, second_ref, first_later_ref, second_later_ref):
    def total(x, half):
        return up(keep_ref, x, half) + up(got_ref, x, half)

    own_ref[0], own_ref[1] = total(0, 0), total(0, 1)
    first_ref[0], first_ref[1] = total(2, 0), total(1, 0)
    second_ref[0], second_ref[1] = total(2, 1), total(3, 1)
    first_later_ref[...] = total(1, 1)
    second_later_ref[...] = total(3, 0)


def add_once_kernel(
    keep_ref, got_ref, first_ref, second_ref, from_first_ref, from_second_ref, own_ref, to_first_ref, far_ref, to_second_ref
):
    ahead = first_ref.shape[0]
    to_first_ref[:ahead] = first_ref[...] + from_second_ref[0]
    to_second_ref[:ahead] = second_ref[...] + from_first_ref[0]
    own_ref[...] = up(keep_ref, 0) + up(got_ref, 0)
    to_first_ref[ahead:] = up(keep_ref, 1) + up(got_ref, 1)
    far_ref[...] = up(keep_ref, 2) + up(got_ref, 2)
    to_second_ref[ahead:] = up(keep_ref, 3) + up(got_ref, 3)


def fold_kernel(first_ref, second_ref, from_first_ref, from_second_ref, to_first_ref, to_second_ref):
    to_first_ref[...] = first_ref[...] + from_second_ref[0]
    to_second_ref[...] = second_ref[...] + from_first_ref[0]


def halves(own_ref, from_first_ref, from_second_ref, later_first_ref, later_second_ref):
    first = own_ref[0] + from_first_ref[1] + later_second_ref[...]
    second = own_ref[1] + from_second_ref[1] + later_first_ref[...]
    return first, second


def node_pairs_kernel(own_ref, from_first_ref, from_second_ref, later_first_ref, later_second_ref, stay_ref, go_ref):
    stay_ref[...], go_ref[...] = halves(own_ref, from_first_ref, from_second_ref, later_first_ref, later_second_ref)


def nodes_kernel(*refs):
    out_ref = refs[-1]
    own_a_ref, from_first_ref, from_second_ref, own_c_ref, first_ref, second_ref, far_ref, stay_ref, got_ref = refs[:-1]
    ahead = own_a_ref.shape[1]
    a = (
        own_a_ref[0] + from_first_ref[1] + second_ref[:ahead],
        own_a_ref[1] + from_second_ref[1] + first_ref[:ahead],
    )
    a = jnp.concatenate([round_to_step(half).astype(jnp.bfloat16) for half in a], axis=0)
    c = own_c_ref[...] + first_ref[ahead:] + far_ref[...] + second_ref[ahead:]
    b = stay_ref[...] + got_ref[...]
    parts = [a, round_to_step(c).astype(jnp.bfloat16), round_to_step(b).astype(jnp.bfloat16)]
    at = 0
    for part in parts:
        rows = part.shape[0] // OWNERS
        for owner in range(OWNERS):
            out_ref[owner, at : at + rows] = part[owner * rows : (owner + 1) * rows]
        at += rows


def final_kernel(pieces_ref, one_ref, two_ref):
    total = up(pieces_ref, 0)
    for source in range(1, OWNERS):
        total = total + up(pieces_ref, source)
    for block in range(LAYER):
        columns = slice(block * BLOCK, (block + 1) * BLOCK)
        one_ref[:, columns] = total[block * SHARE : (block + 1) * SHARE]
        two_ref[:, columns] = total[(LAYER + block) * SHARE : (LAYER + block + 1) * SHARE]


def start_x(keep, got, after=()):
    rows = keep.shape[2]
    f32 = jnp.float32
    own, first, second, first_later, second_later = tiled_call(
        add_kernel, 4, (keep, got), [((2,), rows, f32)] * 3 + [((), rows, f32)] * 2, after
    )
    return own, first_later, second_later, send(first, TO_FIRST), send(second, TO_SECOND)


def end_x(own, first_later, second_later, from_first, from_second, after=()):
    rows = own.shape[1]
    first, second = tiled_call(
        fold_kernel, 1, (first_later, second_later, from_first, from_second), [((), rows, jnp.float32)] * 2, after
    )
    return (own, from_first, from_second, send(first, TO_FIRST), send(second, TO_SECOND)), (first, second)


def body(hidden_one, upstream_one, hidden_two, upstream_two):
    f32, bf16 = jnp.float32, jnp.bfloat16
    me = lax.axis_index("intra").astype(jnp.int32).reshape(1)

    def pair(keep, got, after=()):
        return tiled_call(pair_kernel, 4, (keep, got), [((4,), keep.shape[1], f32)] * 2, after)

    def halved(array, parts):
        rows = array.size // BLOCK // parts // 2
        return array.reshape(parts, 2, rows, BLOCK)

    keep_b, go_b = gradients(me, hidden_two, upstream_two, tuple(range(LAYER)), False, ROOM[0])
    core_b = send(go_b, TO_CORE)
    keep_a, go_a = gradients(me, hidden_one, upstream_one, tuple(range(FIRST)), True, ROOM[1])
    core_a = send(go_a, TO_CORE)
    b = start_x(halved(keep_b, 4), halved(core_b, 4))
    stay_a, go_a = pair(keep_a, core_a, (b[0],))
    y_a = send(go_a, TO_Y)
    keep_c, go_c = gradients(me, hidden_one, upstream_one, tuple(range(FIRST, LAYER)), True, ROOM[2], (stay_a,))
    core_c = send(go_c, TO_CORE)
    stay_c, go_c = pair(keep_c, core_c)
    y_c = send(go_c, TO_Y)

    b, sent_b = end_x(*b, (go_c,))
    a = start_x(halved(stay_a, 4), halved(y_a, 4), sent_b)
    stay_b, go_b = tiled_call(node_pairs_kernel, 2, b, [((), b[0].shape[1], f32)] * 2, (a[0],))
    y_b = send(go_b, TO_Y)
    rows, ahead = stay_c.shape[1], a[1].shape[0]
    own_c, first, far, second = tiled_call(
        add_once_kernel,
        1,
        (stay_c, y_c, *a[1:]),
        [((), rows, f32), ((), ahead + rows, f32), ((), rows, f32), ((), ahead + rows, f32)],
        (go_b,),
    )
    first, second, far = send(first, TO_FIRST), send(second, TO_SECOND), send(far, TO_FAR)

    node = pl.pallas_call(
        nodes_kernel,
        in_specs=[pl.BlockSpec(memory_space=pltpu.VMEM)] * 9,
        out_specs=pl.BlockSpec(memory_space=pltpu.VMEM),
        out_shape=jax.ShapeDtypeStruct((OWNERS, 2 * LAYER * SHARE, BLOCK), bf16),
        compiler_params=PARAMS,
        cost_estimate=SMALL,
    )(a[0], a[3], a[4], own_c, first, second, far, stay_b, y_b)
    pieces = lax.all_to_all(node, "inter", split_axis=0, concat_axis=0, tiled=True)
    out = jax.ShapeDtypeStruct((SHARE, LAYER * BLOCK), f32)
    vmem = pl.BlockSpec(memory_space=pltpu.VMEM)
    return pl.pallas_call(final_kernel, in_specs=[vmem], out_shape=(out, out))(pieces)


def solution(mesh):
    return jax.shard_map(
        body,
        mesh=mesh,
        in_specs=(
            P(("intra", "inter"), None),
            P(("intra", "inter"), None),
            P(("intra", "inter"), None),
            P(("intra", "inter"), None),
        ),
        out_specs=(P("intra", "inter"), P("intra", "inter")),
        check_vma=False,
    )
```

```python
import functools

import jax
import jax.numpy as jnp
from jax import lax
from jax.experimental import pallas as pl
from jax.experimental.pallas import tpu as pltpu
from jax.sharding import PartitionSpec as P

BLOCK = 128
SHARE = 8
LOWEST = 2.0**-34
X, Y, CORES = 4, 2, 2
OWNERS = 16
STEPS = OWNERS // 2
LAYER = 6
FIRST = 4
ROOM = (50, 32, 32)
SMALL = pl.CostEstimate(flops=1, bytes_accessed=1, transcendentals=0)
PARAMS = pltpu.CompilerParams(vmem_limit_bytes=32 * 2**20)


def node_pairs(move):
    pairs = []
    for x in range(X):
        for y in range(Y):
            for core in range(CORES):
                to_x, to_y, to_core = move(x, y, core)
                pairs.append(((x * Y + y) * CORES + core, (to_x % X * Y + to_y) * CORES + to_core))
    return pairs


TO_CORE = node_pairs(lambda x, y, core: (x, y, 1 - core))
TO_Y = node_pairs(lambda x, y, core: (x, 1 - y, core))
TO_FIRST = node_pairs(lambda x, y, core: (x + 1 - 2 * (x % 2), y, core))
TO_FAR = node_pairs(lambda x, y, core: (x + 2, y, core))
TO_SECOND = node_pairs(lambda x, y, core: (x - 1 + 2 * (x % 2), y, core))


def send(array, pairs):
    return lax.ppermute(array, "intra", pairs)


def round_to_step(values):
    largest = jnp.maximum(jnp.max(jnp.abs(values), axis=-1, keepdims=True), LOWEST)
    gap = largest - largest * (1.0 - 2.0**-24)
    step = gap * 2.0**18
    half = gap * 2.0**17
    shift = gap * (1.5 * 2.0**41)
    nearest = (values + shift) - shift
    return nearest + jnp.where(values - nearest >= half, step, 0.0)


def ordered(hidden, me, along_y_first):
    rows = hidden.shape[1]
    place = lax.broadcasted_iota(jnp.int32, (rows, rows), 0)
    row = lax.broadcasted_iota(jnp.int32, (rows, rows), 1)
    core = place // 64
    if along_y_first:
        y, x = place // 32 % 2, place // 8 % 4
    else:
        x, y = place // 16 % 4, place // 8 % 2
    own_x = me // 4
    x = (own_x + x * (1 - 2 * (own_x % 2)) + X) % X
    y = (y + me // 2) % Y
    core = (core + me) % CORES
    source = ((x * Y + y) * CORES + core) * SHARE + place % SHARE
    chosen = jnp.where(row == source, 1.0, 0.0).astype(jnp.bfloat16)
    return lax.dot_general(
        chosen, hidden, (((1,), (1,)), ((), ())), preferred_element_type=jnp.float32
    ).astype(jnp.bfloat16)


def gradient_kernel(share, along_y_first, waits, streamed, me_ref, hidden_ref, upstream_ref, *refs):
    refs = refs[waits:]
    keep_ref, send_ref = refs[:2]
    rows = 2 * SHARE * len(share)
    width = len(share) * BLOCK

    def column(step, owner, block):
        return pl.multiple_of(((step * 2 + owner) * LAYER + share[block]) * BLOCK, BLOCK)

    def copies(step):
        found = []
        for owner in range(2):
            place, arrived = refs[2:]
            source = upstream_ref.at[:, pl.ds(column(step, owner, 0), width)]
            found.append(pltpu.make_async_copy(source, place.at[step, owner], arrived.at[step, owner]))
        return found

    if streamed:
        for step in range(STEPS):
            for copy in copies(step):
                copy.start()
    left = ordered(hidden_ref[...], me_ref[0], along_y_first)

    def one_step(step, carry):
        if streamed:
            for copy in copies(step):
                copy.wait()
        blocks = [(owner, block) for owner in range(2) for block in range(len(share))]
        for pair in range(len(share)):
            both = []
            for owner, block in blocks[2 * pair : 2 * pair + 2]:
                if streamed:
                    upstream = refs[2][step, owner, :, block * BLOCK : (block + 1) * BLOCK]
                else:
                    upstream = upstream_ref[:, pl.ds(column(step, owner, block), BLOCK)]
                grad = jnp.dot(left, upstream, preferred_element_type=jnp.float32)
                both.append(round_to_step(grad).reshape(16, SHARE, BLOCK))
            both = jnp.concatenate(both, axis=1).astype(jnp.bfloat16)
            at = pl.ds(pl.multiple_of(step * rows + pair * 2 * SHARE, 2 * SHARE), 2 * SHARE)
            keep_ref[:, at, :] = both[:8]
            send_ref[:, at, :] = both[8:]
        return carry

    lax.fori_loop(0, STEPS, one_step, 0)


def gradients(me, hidden, upstream, share, along_y_first, room, streamed, after=()):
    tokens = upstream.shape[0]
    out = jax.ShapeDtypeStruct((8, OWNERS * len(share) * SHARE, BLOCK), jnp.bfloat16)
    scratch = [
        pltpu.VMEM((STEPS, 2, tokens, len(share) * BLOCK), jnp.bfloat16),
        pltpu.SemaphoreType.DMA((STEPS, 2)),
    ]
    return pl.pallas_call(
        functools.partial(gradient_kernel, share, along_y_first, len(after), streamed),
        in_specs=[
            pl.BlockSpec(memory_space=pltpu.SMEM),
            pl.BlockSpec(memory_space=pltpu.VMEM),
            pl.BlockSpec(memory_space=pltpu.HBM if streamed else pltpu.VMEM),
        ]
        + [pl.BlockSpec(memory_space=pl.ANY)] * len(after),
        out_specs=[pl.BlockSpec(memory_space=pltpu.VMEM)] * 2,
        out_shape=[out, out],
        scratch_shapes=scratch if streamed else [],
        compiler_params=pltpu.CompilerParams(vmem_limit_bytes=room * 2**20),
        cost_estimate=SMALL,
    )(me, hidden, upstream, *after)


def tiled_call(kernel, steps, ins, outs, after=()):
    shapes = [jax.ShapeDtypeStruct(tuple(lead) + (rows, BLOCK), dtype) for lead, rows, dtype in outs]

    def view(ref, step):
        tile = ref.shape[-2] // steps
        rows = pl.ds(pl.multiple_of(step * tile, tile), tile)
        return ref.at[(slice(None),) * (len(ref.shape) - 2) + (rows, slice(None))]

    def whole(*refs):
        used = refs[: len(ins)] + refs[len(ins) + len(after) :]

        def one_step(step, carry):
            kernel(*[view(ref, step) for ref in used])
            return carry

        lax.fori_loop(0, steps, one_step, 0)

    return pl.pallas_call(
        whole if steps > 1 else lambda *refs: kernel(*refs[: len(ins)], *refs[len(ins) + len(after) :]),
        in_specs=[pl.BlockSpec(memory_space=pltpu.VMEM)] * len(ins)
        + [pl.BlockSpec(memory_space=pl.ANY)] * len(after),
        out_specs=[pl.BlockSpec(memory_space=pltpu.VMEM)] * len(shapes),
        out_shape=shapes,
        compiler_params=PARAMS,
        cost_estimate=SMALL,
    )(*ins, *after)


def up(ref, *index):
    return ref[index].astype(jnp.float32) if index else ref[...].astype(jnp.float32)


def pair_kernel(keep_ref, got_ref, stay_ref, go_ref):
    for part in range(4):
        stay_ref[part] = up(keep_ref, part) + up(got_ref, part)
        go_ref[part] = up(keep_ref, part + 4) + up(got_ref, part + 4)


def add_kernel(keep_ref, got_ref, own_ref, first_ref, second_ref, first_later_ref, second_later_ref):
    def total(x, half):
        return up(keep_ref, x, half) + up(got_ref, x, half)

    own_ref[0], own_ref[1] = total(0, 0), total(0, 1)
    first_ref[0], first_ref[1] = total(2, 0), total(1, 0)
    second_ref[0], second_ref[1] = total(2, 1), total(3, 1)
    first_later_ref[...] = total(1, 1)
    second_later_ref[...] = total(3, 0)


def add_once_kernel(
    keep_ref, got_ref, first_ref, second_ref, from_first_ref, from_second_ref, own_ref, to_first_ref, far_ref, to_second_ref
):
    ahead = first_ref.shape[0]
    to_first_ref[:ahead] = first_ref[...] + from_second_ref[0]
    to_second_ref[:ahead] = second_ref[...] + from_first_ref[0]
    own_ref[...] = up(keep_ref, 0) + up(got_ref, 0)
    to_first_ref[ahead:] = up(keep_ref, 1) + up(got_ref, 1)
    far_ref[...] = up(keep_ref, 2) + up(got_ref, 2)
    to_second_ref[ahead:] = up(keep_ref, 3) + up(got_ref, 3)


def fold_kernel(first_ref, second_ref, from_first_ref, from_second_ref, to_first_ref, to_second_ref):
    to_first_ref[...] = first_ref[...] + from_second_ref[0]
    to_second_ref[...] = second_ref[...] + from_first_ref[0]


def halves(own_ref, from_first_ref, from_second_ref, later_first_ref, later_second_ref):
    first = own_ref[0] + from_first_ref[1] + later_second_ref[...]
    second = own_ref[1] + from_second_ref[1] + later_first_ref[...]
    return first, second


def node_pairs_kernel(own_ref, from_first_ref, from_second_ref, later_first_ref, later_second_ref, stay_ref, go_ref):
    stay_ref[...], go_ref[...] = halves(own_ref, from_first_ref, from_second_ref, later_first_ref, later_second_ref)


def nodes_kernel(*refs):
    out_ref = refs[-1]
    own_a_ref, from_first_ref, from_second_ref, own_c_ref, first_ref, second_ref, far_ref, stay_ref, got_ref = refs[:-1]
    ahead = own_a_ref.shape[1]
    a = (
        own_a_ref[0] + from_first_ref[1] + second_ref[:ahead],
        own_a_ref[1] + from_second_ref[1] + first_ref[:ahead],
    )
    a = jnp.concatenate([round_to_step(half).astype(jnp.bfloat16) for half in a], axis=0)
    c = own_c_ref[...] + first_ref[ahead:] + far_ref[...] + second_ref[ahead:]
    b = stay_ref[...] + got_ref[...]
    parts = [a, round_to_step(c).astype(jnp.bfloat16), round_to_step(b).astype(jnp.bfloat16)]
    at = 0
    for part in parts:
        rows = part.shape[0] // OWNERS
        for owner in range(OWNERS):
            out_ref[owner, at : at + rows] = part[owner * rows : (owner + 1) * rows]
        at += rows


def final_kernel(pieces_ref, one_ref, two_ref):
    total = up(pieces_ref, 0)
    for source in range(1, OWNERS):
        total = total + up(pieces_ref, source)
    for block in range(LAYER):
        columns = slice(block * BLOCK, (block + 1) * BLOCK)
        one_ref[:, columns] = total[block * SHARE : (block + 1) * SHARE]
        two_ref[:, columns] = total[(LAYER + block) * SHARE : (LAYER + block + 1) * SHARE]


def start_x(keep, got, after=()):
    rows = keep.shape[2]
    f32 = jnp.float32
    own, first, second, first_later, second_later = tiled_call(
        add_kernel, 4, (keep, got), [((2,), rows, f32)] * 3 + [((), rows, f32)] * 2, after
    )
    return own, first_later, second_later, send(first, TO_FIRST), send(second, TO_SECOND)


def end_x(own, first_later, second_later, from_first, from_second, after=()):
    rows = own.shape[1]
    first, second = tiled_call(
        fold_kernel, 1, (first_later, second_later, from_first, from_second), [((), rows, jnp.float32)] * 2, after
    )
    return (own, from_first, from_second, send(first, TO_FIRST), send(second, TO_SECOND)), (first, second)


def body(hidden_one, upstream_one, hidden_two, upstream_two):
    f32, bf16 = jnp.float32, jnp.bfloat16
    me = lax.axis_index("intra").astype(jnp.int32).reshape(1)

    def pair(keep, got, after=()):
        return tiled_call(pair_kernel, 4, (keep, got), [((4,), keep.shape[1], f32)] * 2, after)

    def halved(array, parts):
        rows = array.size // BLOCK // parts // 2
        return array.reshape(parts, 2, rows, BLOCK)

    keep_b, go_b = gradients(me, hidden_two, upstream_two, tuple(range(LAYER)), False, ROOM[0], True)
    core_b = send(go_b, TO_CORE)
    keep_a, go_a = gradients(me, hidden_one, upstream_one, tuple(range(FIRST)), True, ROOM[1], False)
    core_a = send(go_a, TO_CORE)
    b = start_x(halved(keep_b, 4), halved(core_b, 4))
    stay_a, go_a = pair(keep_a, core_a, (b[0],))
    y_a = send(go_a, TO_Y)
    keep_c, go_c = gradients(me, hidden_one, upstream_one, tuple(range(FIRST, LAYER)), True, ROOM[2], False, (stay_a,))
    core_c = send(go_c, TO_CORE)
    stay_c, go_c = pair(keep_c, core_c)
    y_c = send(go_c, TO_Y)

    b, sent_b = end_x(*b, (go_c,))
    a = start_x(halved(stay_a, 4), halved(y_a, 4), sent_b)
    stay_b, go_b = tiled_call(node_pairs_kernel, 2, b, [((), b[0].shape[1], f32)] * 2, (a[0],))
    y_b = send(go_b, TO_Y)
    rows, ahead = stay_c.shape[1], a[1].shape[0]
    own_c, first, far, second = tiled_call(
        add_once_kernel,
        1,
        (stay_c, y_c, *a[1:]),
        [((), rows, f32), ((), ahead + rows, f32), ((), rows, f32), ((), ahead + rows, f32)],
        (go_b,),
    )
    first, second, far = send(first, TO_FIRST), send(second, TO_SECOND), send(far, TO_FAR)

    node = pl.pallas_call(
        nodes_kernel,
        in_specs=[pl.BlockSpec(memory_space=pltpu.VMEM)] * 9,
        out_specs=pl.BlockSpec(memory_space=pltpu.VMEM),
        out_shape=jax.ShapeDtypeStruct((OWNERS, 2 * LAYER * SHARE, BLOCK), bf16),
        compiler_params=PARAMS,
        cost_estimate=SMALL,
    )(a[0], a[3], a[4], own_c, first, second, far, stay_b, y_b)
    pieces = lax.all_to_all(node, "inter", split_axis=0, concat_axis=0, tiled=True)
    out = jax.ShapeDtypeStruct((SHARE, LAYER * BLOCK), f32)
    vmem = pl.BlockSpec(memory_space=pltpu.VMEM)
    return pl.pallas_call(final_kernel, in_specs=[vmem], out_shape=(out, out))(pieces)


def solution(mesh):
    return jax.shard_map(
        body,
        mesh=mesh,
        in_specs=(
            P(("intra", "inter"), None),
            P(("intra", "inter"), None),
            P(("intra", "inter"), None),
            P(("intra", "inter"), None),
        ),
        out_specs=(P("intra", "inter"), P("intra", "inter")),
        check_vma=False,
    )
```

```python
import functools

import jax
import jax.numpy as jnp
from jax import lax
from jax.experimental import pallas as pl
from jax.experimental.pallas import tpu as pltpu
from jax.sharding import PartitionSpec as P

BLOCK = 128
SHARE = 8
LOWEST = 2.0**-34
X, Y, CORES = 4, 2, 2
OWNERS = 16
STEPS = OWNERS // 2
WAITS = ((0, 1), (1, 3), (3, STEPS))
LAYER = 6
FIRST = 4
ROOM = (50, 32, 32)
SMALL = pl.CostEstimate(flops=1, bytes_accessed=1, transcendentals=0)
PARAMS = pltpu.CompilerParams(vmem_limit_bytes=32 * 2**20)


def node_pairs(move):
    pairs = []
    for x in range(X):
        for y in range(Y):
            for core in range(CORES):
                to_x, to_y, to_core = move(x, y, core)
                pairs.append(((x * Y + y) * CORES + core, (to_x % X * Y + to_y) * CORES + to_core))
    return pairs


TO_CORE = node_pairs(lambda x, y, core: (x, y, 1 - core))
TO_Y = node_pairs(lambda x, y, core: (x, 1 - y, core))
TO_FIRST = node_pairs(lambda x, y, core: (x + 1 - 2 * (x % 2), y, core))
TO_FAR = node_pairs(lambda x, y, core: (x + 2, y, core))
TO_SECOND = node_pairs(lambda x, y, core: (x - 1 + 2 * (x % 2), y, core))


def send(array, pairs):
    return lax.ppermute(array, "intra", pairs)


def round_to_step(values):
    largest = jnp.maximum(jnp.max(jnp.abs(values), axis=-1, keepdims=True), LOWEST)
    gap = largest - largest * (1.0 - 2.0**-24)
    step = gap * 2.0**18
    half = gap * 2.0**17
    shift = gap * (1.5 * 2.0**41)
    nearest = (values + shift) - shift
    return nearest + jnp.where(values - nearest >= half, step, 0.0)


def ordered(hidden, me, along_y_first):
    rows = hidden.shape[1]
    place = lax.broadcasted_iota(jnp.int32, (rows, rows), 0)
    row = lax.broadcasted_iota(jnp.int32, (rows, rows), 1)
    core = place // 64
    if along_y_first:
        y, x = place // 32 % 2, place // 8 % 4
    else:
        x, y = place // 16 % 4, place // 8 % 2
    own_x = me // 4
    x = (own_x + x * (1 - 2 * (own_x % 2)) + X) % X
    y = (y + me // 2) % Y
    core = (core + me) % CORES
    source = ((x * Y + y) * CORES + core) * SHARE + place % SHARE
    chosen = jnp.where(row == source, 1.0, 0.0).astype(jnp.bfloat16)
    return lax.dot_general(
        chosen, hidden, (((1,), (1,)), ((), ())), preferred_element_type=jnp.float32
    ).astype(jnp.bfloat16)


def gradient_kernel(share, along_y_first, waits, streamed, me_ref, hidden_ref, upstream_ref, *refs):
    refs = refs[waits:]
    keep_ref, send_ref = refs[:2]
    rows = 2 * SHARE * len(share)
    width = len(share) * BLOCK

    def column(step, owner, block):
        start = ((step * 2 + owner) * LAYER + share[block]) * BLOCK
        return start if isinstance(start, int) else pl.multiple_of(start, BLOCK)

    def copies(step):
        found = []
        for owner in range(2):
            place, arrived = refs[2:]
            source = upstream_ref.at[:, pl.ds(column(step, owner, 0), width)]
            found.append(pltpu.make_async_copy(source, place.at[step, owner], arrived.at[step, owner]))
        return found

    if streamed:
        for step in range(STEPS):
            for copy in copies(step):
                copy.start()
    left = ordered(hidden_ref[...], me_ref[0], along_y_first)

    def one_step(step, carry):
        blocks = [(owner, block) for owner in range(2) for block in range(len(share))]
        for pair in range(len(share)):
            both = []
            for owner, block in blocks[2 * pair : 2 * pair + 2]:
                if streamed:
                    upstream = refs[2][step, owner, :, block * BLOCK : (block + 1) * BLOCK]
                else:
                    upstream = upstream_ref[:, pl.ds(column(step, owner, block), BLOCK)]
                grad = jnp.dot(left, upstream, preferred_element_type=jnp.float32)
                both.append(round_to_step(grad).reshape(16, SHARE, BLOCK))
            both = jnp.concatenate(both, axis=1).astype(jnp.bfloat16)
            start = step * rows + pair * 2 * SHARE
            at = pl.ds(start if isinstance(start, int) else pl.multiple_of(start, 2 * SHARE), 2 * SHARE)
            keep_ref[:, at, :] = both[:8]
            send_ref[:, at, :] = both[8:]
        return carry

    if streamed:
        for begin, end in WAITS:
            for step in range(begin, end):
                for copy in copies(step):
                    copy.wait()
            for step in range(begin, end):
                one_step(step, 0)
    else:
        lax.fori_loop(0, STEPS, one_step, 0, unroll=4)


def gradients(me, hidden, upstream, share, along_y_first, room, streamed, after=()):
    tokens = upstream.shape[0]
    out = jax.ShapeDtypeStruct((8, OWNERS * len(share) * SHARE, BLOCK), jnp.bfloat16)
    scratch = [
        pltpu.VMEM((STEPS, 2, tokens, len(share) * BLOCK), jnp.bfloat16),
        pltpu.SemaphoreType.DMA((STEPS, 2)),
    ]
    return pl.pallas_call(
        functools.partial(gradient_kernel, share, along_y_first, len(after), streamed),
        in_specs=[
            pl.BlockSpec(memory_space=pltpu.SMEM),
            pl.BlockSpec(memory_space=pltpu.VMEM),
            pl.BlockSpec(memory_space=pltpu.HBM if streamed else pltpu.VMEM),
        ]
        + [pl.BlockSpec(memory_space=pl.ANY)] * len(after),
        out_specs=[pl.BlockSpec(memory_space=pltpu.VMEM)] * 2,
        out_shape=[out, out],
        scratch_shapes=scratch if streamed else [],
        compiler_params=pltpu.CompilerParams(vmem_limit_bytes=room * 2**20),
        cost_estimate=SMALL,
    )(me, hidden, upstream, *after)


def tiled_call(kernel, steps, ins, outs, after=()):
    shapes = [jax.ShapeDtypeStruct(tuple(lead) + (rows, BLOCK), dtype) for lead, rows, dtype in outs]

    def view(ref, step):
        tile = ref.shape[-2] // steps
        rows = pl.ds(pl.multiple_of(step * tile, tile), tile)
        return ref.at[(slice(None),) * (len(ref.shape) - 2) + (rows, slice(None))]

    def whole(*refs):
        used = refs[: len(ins)] + refs[len(ins) + len(after) :]

        def one_step(step, carry):
            kernel(*[view(ref, step) for ref in used])
            return carry

        lax.fori_loop(0, steps, one_step, 0)

    return pl.pallas_call(
        whole if steps > 1 else lambda *refs: kernel(*refs[: len(ins)], *refs[len(ins) + len(after) :]),
        in_specs=[pl.BlockSpec(memory_space=pltpu.VMEM)] * len(ins)
        + [pl.BlockSpec(memory_space=pl.ANY)] * len(after),
        out_specs=[pl.BlockSpec(memory_space=pltpu.VMEM)] * len(shapes),
        out_shape=shapes,
        compiler_params=PARAMS,
        cost_estimate=SMALL,
    )(*ins, *after)


def up(ref, *index):
    return ref[index].astype(jnp.float32) if index else ref[...].astype(jnp.float32)


def pair_kernel(keep_ref, got_ref, stay_ref, go_ref):
    for part in range(4):
        stay_ref[part] = up(keep_ref, part) + up(got_ref, part)
        go_ref[part] = up(keep_ref, part + 4) + up(got_ref, part + 4)


def add_kernel(keep_ref, got_ref, own_ref, first_ref, second_ref, first_later_ref, second_later_ref):
    def total(x, half):
        return up(keep_ref, x, half) + up(got_ref, x, half)

    own_ref[0], own_ref[1] = total(0, 0), total(0, 1)
    first_ref[0], first_ref[1] = total(2, 0), total(1, 0)
    second_ref[0], second_ref[1] = total(2, 1), total(3, 1)
    first_later_ref[...] = total(1, 1)
    second_later_ref[...] = total(3, 0)


def add_once_kernel(
    keep_ref, got_ref, first_ref, second_ref, from_first_ref, from_second_ref, own_ref, to_first_ref, far_ref, to_second_ref
):
    ahead = first_ref.shape[0]
    to_first_ref[:ahead] = first_ref[...] + from_second_ref[0]
    to_second_ref[:ahead] = second_ref[...] + from_first_ref[0]
    own_ref[...] = up(keep_ref, 0) + up(got_ref, 0)
    to_first_ref[ahead:] = up(keep_ref, 1) + up(got_ref, 1)
    far_ref[...] = up(keep_ref, 2) + up(got_ref, 2)
    to_second_ref[ahead:] = up(keep_ref, 3) + up(got_ref, 3)


def fold_kernel(first_ref, second_ref, from_first_ref, from_second_ref, to_first_ref, to_second_ref):
    to_first_ref[...] = first_ref[...] + from_second_ref[0]
    to_second_ref[...] = second_ref[...] + from_first_ref[0]


def halves(own_ref, from_first_ref, from_second_ref, later_first_ref, later_second_ref):
    first = own_ref[0] + from_first_ref[1] + later_second_ref[...]
    second = own_ref[1] + from_second_ref[1] + later_first_ref[...]
    return first, second


def node_pairs_kernel(own_ref, from_first_ref, from_second_ref, later_first_ref, later_second_ref, stay_ref, go_ref):
    stay_ref[...], go_ref[...] = halves(own_ref, from_first_ref, from_second_ref, later_first_ref, later_second_ref)


def nodes_kernel(*refs):
    out_ref = refs[-1]
    own_a_ref, from_first_ref, from_second_ref, own_c_ref, first_ref, second_ref, far_ref, stay_ref, got_ref = refs[:-1]
    ahead = own_a_ref.shape[1]
    a = (
        own_a_ref[0] + from_first_ref[1] + second_ref[:ahead],
        own_a_ref[1] + from_second_ref[1] + first_ref[:ahead],
    )
    a = jnp.concatenate([round_to_step(half).astype(jnp.bfloat16) for half in a], axis=0)
    c = own_c_ref[...] + first_ref[ahead:] + far_ref[...] + second_ref[ahead:]
    b = stay_ref[...] + got_ref[...]
    parts = [a, round_to_step(c).astype(jnp.bfloat16), round_to_step(b).astype(jnp.bfloat16)]
    at = 0
    for part in parts:
        rows = part.shape[0] // OWNERS
        for owner in range(OWNERS):
            out_ref[owner, at : at + rows] = part[owner * rows : (owner + 1) * rows]
        at += rows


def final_kernel(pieces_ref, one_ref, two_ref):
    total = up(pieces_ref, 0)
    for source in range(1, OWNERS):
        total = total + up(pieces_ref, source)
    for block in range(LAYER):
        columns = slice(block * BLOCK, (block + 1) * BLOCK)
        one_ref[:, columns] = total[block * SHARE : (block + 1) * SHARE]
        two_ref[:, columns] = total[(LAYER + block) * SHARE : (LAYER + block + 1) * SHARE]


def start_x(keep, got, after=()):
    rows = keep.shape[2]
    f32 = jnp.float32
    own, first, second, first_later, second_later = tiled_call(
        add_kernel, 4, (keep, got), [((2,), rows, f32)] * 3 + [((), rows, f32)] * 2, after
    )
    return own, first_later, second_later, send(first, TO_FIRST), send(second, TO_SECOND)


def end_x(own, first_later, second_later, from_first, from_second, after=()):
    rows = own.shape[1]
    first, second = tiled_call(
        fold_kernel, 1, (first_later, second_later, from_first, from_second), [((), rows, jnp.float32)] * 2, after
    )
    return (own, from_first, from_second, send(first, TO_FIRST), send(second, TO_SECOND)), (first, second)


def body(hidden_one, upstream_one, hidden_two, upstream_two):
    f32, bf16 = jnp.float32, jnp.bfloat16
    me = lax.axis_index("intra").astype(jnp.int32).reshape(1)

    def pair(keep, got, after=()):
        return tiled_call(pair_kernel, 4, (keep, got), [((4,), keep.shape[1], f32)] * 2, after)

    def halved(array, parts):
        rows = array.size // BLOCK // parts // 2
        return array.reshape(parts, 2, rows, BLOCK)

    keep_b, go_b = gradients(me, hidden_two, upstream_two, tuple(range(LAYER)), False, ROOM[0], True)
    core_b = send(go_b, TO_CORE)
    keep_a, go_a = gradients(me, hidden_one, upstream_one, tuple(range(FIRST)), True, ROOM[1], False)
    core_a = send(go_a, TO_CORE)
    b = start_x(halved(keep_b, 4), halved(core_b, 4))
    stay_a, go_a = pair(keep_a, core_a, (b[0],))
    y_a = send(go_a, TO_Y)
    keep_c, go_c = gradients(me, hidden_one, upstream_one, tuple(range(FIRST, LAYER)), True, ROOM[2], False, (stay_a,))
    core_c = send(go_c, TO_CORE)
    stay_c, go_c = pair(keep_c, core_c)
    y_c = send(go_c, TO_Y)

    b, sent_b = end_x(*b, (go_c,))
    a = start_x(halved(stay_a, 4), halved(y_a, 4), sent_b)
    stay_b, go_b = tiled_call(node_pairs_kernel, 2, b, [((), b[0].shape[1], f32)] * 2, (a[0],))
    y_b = send(go_b, TO_Y)
    rows, ahead = stay_c.shape[1], a[1].shape[0]
    own_c, first, far, second = tiled_call(
        add_once_kernel,
        1,
        (stay_c, y_c, *a[1:]),
        [((), rows, f32), ((), ahead + rows, f32), ((), rows, f32), ((), ahead + rows, f32)],
        (go_b,),
    )
    first, second, far = send(first, TO_FIRST), send(second, TO_SECOND), send(far, TO_FAR)

    node = pl.pallas_call(
        nodes_kernel,
        in_specs=[pl.BlockSpec(memory_space=pltpu.VMEM)] * 9,
        out_specs=pl.BlockSpec(memory_space=pltpu.VMEM),
        out_shape=jax.ShapeDtypeStruct((OWNERS, 2 * LAYER * SHARE, BLOCK), bf16),
        compiler_params=PARAMS,
        cost_estimate=SMALL,
    )(a[0], a[3], a[4], own_c, first, second, far, stay_b, y_b)
    pieces = lax.all_to_all(node, "inter", split_axis=0, concat_axis=0, tiled=True)
    out = jax.ShapeDtypeStruct((SHARE, LAYER * BLOCK), f32)
    vmem = pl.BlockSpec(memory_space=pltpu.VMEM)
    return pl.pallas_call(final_kernel, in_specs=[vmem], out_shape=(out, out))(pieces)


def solution(mesh):
    return jax.shard_map(
        body,
        mesh=mesh,
        in_specs=(
            P(("intra", "inter"), None),
            P(("intra", "inter"), None),
            P(("intra", "inter"), None),
            P(("intra", "inter"), None),
        ),
        out_specs=(P("intra", "inter"), P("intra", "inter")),
        check_vma=False,
    )
```

```python
import functools

import jax
import jax.numpy as jnp
from jax import lax
from jax.experimental import pallas as pl
from jax.experimental.pallas import tpu as pltpu
from jax.sharding import PartitionSpec as P

BLOCK = 128
SHARE = 8
LOWEST = 2.0**-34
X, Y, CORES = 4, 2, 2
OWNERS = 16
STEPS = OWNERS // 2
WAITS = ((0, 2), (2, STEPS))
LAYER = 6
FIRST = 4
ROOM = (50, 32, 32)
SMALL = pl.CostEstimate(flops=1, bytes_accessed=1, transcendentals=0)
PARAMS = pltpu.CompilerParams(vmem_limit_bytes=32 * 2**20)


def node_pairs(move):
    pairs = []
    for x in range(X):
        for y in range(Y):
            for core in range(CORES):
                to_x, to_y, to_core = move(x, y, core)
                pairs.append(((x * Y + y) * CORES + core, (to_x % X * Y + to_y) * CORES + to_core))
    return pairs


TO_CORE = node_pairs(lambda x, y, core: (x, y, 1 - core))
TO_Y = node_pairs(lambda x, y, core: (x, 1 - y, core))
TO_FIRST = node_pairs(lambda x, y, core: (x + 1 - 2 * (x % 2), y, core))
TO_FAR = node_pairs(lambda x, y, core: (x + 2, y, core))
TO_SECOND = node_pairs(lambda x, y, core: (x - 1 + 2 * (x % 2), y, core))


def send(array, pairs):
    return lax.ppermute(array, "intra", pairs)


def round_to_step(values):
    largest = jnp.maximum(jnp.max(jnp.abs(values), axis=-1, keepdims=True), LOWEST)
    gap = largest - largest * (1.0 - 2.0**-24)
    step = gap * 2.0**18
    half = gap * 2.0**17
    shift = gap * (1.5 * 2.0**41)
    nearest = (values + shift) - shift
    return nearest + jnp.where(values - nearest >= half, step, 0.0)


def ordered(hidden, me, along_y_first):
    rows = hidden.shape[1]
    place = lax.broadcasted_iota(jnp.int32, (rows, rows), 0)
    row = lax.broadcasted_iota(jnp.int32, (rows, rows), 1)
    core = place // 64
    if along_y_first:
        y, x = place // 32 % 2, place // 8 % 4
    else:
        x, y = place // 16 % 4, place // 8 % 2
    own_x = me // 4
    x = (own_x + x * (1 - 2 * (own_x % 2)) + X) % X
    y = (y + me // 2) % Y
    core = (core + me) % CORES
    source = ((x * Y + y) * CORES + core) * SHARE + place % SHARE
    chosen = jnp.where(row == source, 1.0, 0.0).astype(jnp.bfloat16)
    return lax.dot_general(
        chosen, hidden, (((1,), (1,)), ((), ())), preferred_element_type=jnp.float32
    ).astype(jnp.bfloat16)


def gradient_kernel(share, along_y_first, waits, streamed, me_ref, hidden_ref, upstream_ref, *refs):
    refs = refs[waits:]
    keep_ref, send_ref = refs[:2]
    rows = 2 * SHARE * len(share)
    width = len(share) * BLOCK

    def column(step, owner, block):
        start = ((step * 2 + owner) * LAYER + share[block]) * BLOCK
        return start if isinstance(start, int) else pl.multiple_of(start, BLOCK)

    def copies(step):
        found = []
        for owner in range(2):
            place, arrived = refs[2:]
            source = upstream_ref.at[:, pl.ds(column(step, owner, 0), width)]
            found.append(pltpu.make_async_copy(source, place.at[step, owner], arrived.at[step, owner]))
        return found

    if streamed:
        for step in range(STEPS):
            for copy in copies(step):
                copy.start()
    left = ordered(hidden_ref[...], me_ref[0], along_y_first)

    def one_step(step, carry):
        blocks = [(owner, block) for owner in range(2) for block in range(len(share))]
        for pair in range(len(share)):
            both = []
            for owner, block in blocks[2 * pair : 2 * pair + 2]:
                if streamed:
                    upstream = refs[2][step, owner, :, block * BLOCK : (block + 1) * BLOCK]
                else:
                    upstream = upstream_ref[:, pl.ds(column(step, owner, block), BLOCK)]
                grad = jnp.dot(left, upstream, preferred_element_type=jnp.float32)
                both.append(round_to_step(grad).reshape(16, SHARE, BLOCK))
            both = jnp.concatenate(both, axis=1).astype(jnp.bfloat16)
            start = step * rows + pair * 2 * SHARE
            at = pl.ds(start if isinstance(start, int) else pl.multiple_of(start, 2 * SHARE), 2 * SHARE)
            keep_ref[:, at, :] = both[:8]
            send_ref[:, at, :] = both[8:]
        return carry

    if streamed:
        for begin, end in WAITS:
            for step in range(begin, end):
                for copy in copies(step):
                    copy.wait()
            for step in range(begin, end):
                one_step(step, 0)
    else:
        lax.fori_loop(0, STEPS, one_step, 0, unroll=True)


def gradients(me, hidden, upstream, share, along_y_first, room, streamed, after=()):
    tokens = upstream.shape[0]
    out = jax.ShapeDtypeStruct((8, OWNERS * len(share) * SHARE, BLOCK), jnp.bfloat16)
    scratch = [
        pltpu.VMEM((STEPS, 2, tokens, len(share) * BLOCK), jnp.bfloat16),
        pltpu.SemaphoreType.DMA((STEPS, 2)),
    ]
    return pl.pallas_call(
        functools.partial(gradient_kernel, share, along_y_first, len(after), streamed),
        in_specs=[
            pl.BlockSpec(memory_space=pltpu.SMEM),
            pl.BlockSpec(memory_space=pltpu.VMEM),
            pl.BlockSpec(memory_space=pltpu.HBM if streamed else pltpu.VMEM),
        ]
        + [pl.BlockSpec(memory_space=pl.ANY)] * len(after),
        out_specs=[pl.BlockSpec(memory_space=pltpu.VMEM)] * 2,
        out_shape=[out, out],
        scratch_shapes=scratch if streamed else [],
        compiler_params=pltpu.CompilerParams(vmem_limit_bytes=room * 2**20),
        cost_estimate=SMALL,
    )(me, hidden, upstream, *after)


def tiled_call(kernel, steps, ins, outs, after=()):
    shapes = [jax.ShapeDtypeStruct(tuple(lead) + (rows, BLOCK), dtype) for lead, rows, dtype in outs]

    def view(ref, step):
        tile = ref.shape[-2] // steps
        rows = pl.ds(pl.multiple_of(step * tile, tile), tile)
        return ref.at[(slice(None),) * (len(ref.shape) - 2) + (rows, slice(None))]

    def whole(*refs):
        used = refs[: len(ins)] + refs[len(ins) + len(after) :]

        def one_step(step, carry):
            kernel(*[view(ref, step) for ref in used])
            return carry

        lax.fori_loop(0, steps, one_step, 0)

    return pl.pallas_call(
        whole if steps > 1 else lambda *refs: kernel(*refs[: len(ins)], *refs[len(ins) + len(after) :]),
        in_specs=[pl.BlockSpec(memory_space=pltpu.VMEM)] * len(ins)
        + [pl.BlockSpec(memory_space=pl.ANY)] * len(after),
        out_specs=[pl.BlockSpec(memory_space=pltpu.VMEM)] * len(shapes),
        out_shape=shapes,
        compiler_params=PARAMS,
        cost_estimate=SMALL,
    )(*ins, *after)


def up(ref, *index):
    return ref[index].astype(jnp.float32) if index else ref[...].astype(jnp.float32)


def pair_kernel(keep_ref, got_ref, stay_ref, go_ref):
    for part in range(4):
        stay_ref[part] = up(keep_ref, part) + up(got_ref, part)
        go_ref[part] = up(keep_ref, part + 4) + up(got_ref, part + 4)


def add_kernel(keep_ref, got_ref, own_ref, first_ref, second_ref, first_later_ref, second_later_ref):
    def total(x, half):
        return up(keep_ref, x, half) + up(got_ref, x, half)

    own_ref[0], own_ref[1] = total(0, 0), total(0, 1)
    first_ref[0], first_ref[1] = total(2, 0), total(1, 0)
    second_ref[0], second_ref[1] = total(2, 1), total(3, 1)
    first_later_ref[...] = total(1, 1)
    second_later_ref[...] = total(3, 0)


def add_once_kernel(
    keep_ref, got_ref, first_ref, second_ref, from_first_ref, from_second_ref, own_ref, to_first_ref, far_ref, to_second_ref
):
    ahead = first_ref.shape[0]
    to_first_ref[:ahead] = first_ref[...] + from_second_ref[0]
    to_second_ref[:ahead] = second_ref[...] + from_first_ref[0]
    own_ref[...] = up(keep_ref, 0) + up(got_ref, 0)
    to_first_ref[ahead:] = up(keep_ref, 1) + up(got_ref, 1)
    far_ref[...] = up(keep_ref, 2) + up(got_ref, 2)
    to_second_ref[ahead:] = up(keep_ref, 3) + up(got_ref, 3)


def fold_kernel(first_ref, second_ref, from_first_ref, from_second_ref, to_first_ref, to_second_ref):
    to_first_ref[...] = first_ref[...] + from_second_ref[0]
    to_second_ref[...] = second_ref[...] + from_first_ref[0]


def halves(own_ref, from_first_ref, from_second_ref, later_first_ref, later_second_ref):
    first = own_ref[0] + from_first_ref[1] + later_second_ref[...]
    second = own_ref[1] + from_second_ref[1] + later_first_ref[...]
    return first, second


def node_pairs_kernel(own_ref, from_first_ref, from_second_ref, later_first_ref, later_second_ref, stay_ref, go_ref):
    stay_ref[...], go_ref[...] = halves(own_ref, from_first_ref, from_second_ref, later_first_ref, later_second_ref)


def nodes_kernel(*refs):
    out_ref = refs[-1]
    own_a_ref, from_first_ref, from_second_ref, own_c_ref, first_ref, second_ref, far_ref, stay_ref, got_ref = refs[:-1]
    ahead = own_a_ref.shape[1]
    a = (
        own_a_ref[0] + from_first_ref[1] + second_ref[:ahead],
        own_a_ref[1] + from_second_ref[1] + first_ref[:ahead],
    )
    a = jnp.concatenate([round_to_step(half).astype(jnp.bfloat16) for half in a], axis=0)
    c = own_c_ref[...] + first_ref[ahead:] + far_ref[...] + second_ref[ahead:]
    b = stay_ref[...] + got_ref[...]
    parts = [a, round_to_step(c).astype(jnp.bfloat16), round_to_step(b).astype(jnp.bfloat16)]
    at = 0
    for part in parts:
        rows = part.shape[0] // OWNERS
        for owner in range(OWNERS):
            out_ref[owner, at : at + rows] = part[owner * rows : (owner + 1) * rows]
        at += rows


def final_kernel(pieces_ref, one_ref, two_ref):
    total = up(pieces_ref, 0)
    for source in range(1, OWNERS):
        total = total + up(pieces_ref, source)
    for block in range(LAYER):
        columns = slice(block * BLOCK, (block + 1) * BLOCK)
        one_ref[:, columns] = total[block * SHARE : (block + 1) * SHARE]
        two_ref[:, columns] = total[(LAYER + block) * SHARE : (LAYER + block + 1) * SHARE]


def start_x(keep, got, after=()):
    rows = keep.shape[2]
    f32 = jnp.float32
    own, first, second, first_later, second_later = tiled_call(
        add_kernel, 4, (keep, got), [((2,), rows, f32)] * 3 + [((), rows, f32)] * 2, after
    )
    return own, first_later, second_later, send(first, TO_FIRST), send(second, TO_SECOND)


def end_x(own, first_later, second_later, from_first, from_second, after=()):
    rows = own.shape[1]
    first, second = tiled_call(
        fold_kernel, 1, (first_later, second_later, from_first, from_second), [((), rows, jnp.float32)] * 2, after
    )
    return (own, from_first, from_second, send(first, TO_FIRST), send(second, TO_SECOND)), (first, second)


def body(hidden_one, upstream_one, hidden_two, upstream_two):
    f32, bf16 = jnp.float32, jnp.bfloat16
    me = lax.axis_index("intra").astype(jnp.int32).reshape(1)

    def pair(keep, got, after=()):
        return tiled_call(pair_kernel, 4, (keep, got), [((4,), keep.shape[1], f32)] * 2, after)

    def halved(array, parts):
        rows = array.size // BLOCK // parts // 2
        return array.reshape(parts, 2, rows, BLOCK)

    keep_b, go_b = gradients(me, hidden_two, upstream_two, tuple(range(LAYER)), False, ROOM[0], True)
    core_b = send(go_b, TO_CORE)
    keep_a, go_a = gradients(me, hidden_one, upstream_one, tuple(range(FIRST)), True, ROOM[1], False)
    core_a = send(go_a, TO_CORE)
    b = start_x(halved(keep_b, 4), halved(core_b, 4))
    stay_a, go_a = pair(keep_a, core_a, (b[0],))
    y_a = send(go_a, TO_Y)
    keep_c, go_c = gradients(me, hidden_one, upstream_one, tuple(range(FIRST, LAYER)), True, ROOM[2], False, (stay_a,))
    core_c = send(go_c, TO_CORE)
    stay_c, go_c = pair(keep_c, core_c)
    y_c = send(go_c, TO_Y)

    b, sent_b = end_x(*b, (go_c,))
    a = start_x(halved(stay_a, 4), halved(y_a, 4), sent_b)
    stay_b, go_b = tiled_call(node_pairs_kernel, 2, b, [((), b[0].shape[1], f32)] * 2, (a[0],))
    y_b = send(go_b, TO_Y)
    rows, ahead = stay_c.shape[1], a[1].shape[0]
    own_c, first, far, second = tiled_call(
        add_once_kernel,
        1,
        (stay_c, y_c, *a[1:]),
        [((), rows, f32), ((), ahead + rows, f32), ((), rows, f32), ((), ahead + rows, f32)],
        (go_b,),
    )
    first, second, far = send(first, TO_FIRST), send(second, TO_SECOND), send(far, TO_FAR)

    node = pl.pallas_call(
        nodes_kernel,
        in_specs=[pl.BlockSpec(memory_space=pltpu.VMEM)] * 9,
        out_specs=pl.BlockSpec(memory_space=pltpu.VMEM),
        out_shape=jax.ShapeDtypeStruct((OWNERS, 2 * LAYER * SHARE, BLOCK), bf16),
        compiler_params=PARAMS,
        cost_estimate=SMALL,
    )(a[0], a[3], a[4], own_c, first, second, far, stay_b, y_b)
    pieces = lax.all_to_all(node, "inter", split_axis=0, concat_axis=0, tiled=True)
    out = jax.ShapeDtypeStruct((SHARE, LAYER * BLOCK), f32)
    vmem = pl.BlockSpec(memory_space=pltpu.VMEM)
    return pl.pallas_call(final_kernel, in_specs=[vmem], out_shape=(out, out))(pieces)


def solution(mesh):
    return jax.shard_map(
        body,
        mesh=mesh,
        in_specs=(
            P(("intra", "inter"), None),
            P(("intra", "inter"), None),
            P(("intra", "inter"), None),
            P(("intra", "inter"), None),
        ),
        out_specs=(P("intra", "inter"), P("intra", "inter")),
        check_vma=False,
    )
```

```python
import functools

import jax
import jax.numpy as jnp
from jax import lax
from jax.experimental import pallas as pl
from jax.experimental.pallas import tpu as pltpu
from jax.sharding import PartitionSpec as P

BLOCK = 128
SHARE = 8
LOWEST = 2.0**-34
X, Y, CORES = 4, 2, 2
OWNERS = 16
STEPS = OWNERS // 2
WAITS = ((0, 2), (2, STEPS))
LAYER = 6
FIRST = 4
ROOM = (50, 32, 32)
SMALL = pl.CostEstimate(flops=1, bytes_accessed=1, transcendentals=0)
PARAMS = pltpu.CompilerParams(vmem_limit_bytes=32 * 2**20)


def node_pairs(move):
    pairs = []
    for x in range(X):
        for y in range(Y):
            for core in range(CORES):
                to_x, to_y, to_core = move(x, y, core)
                pairs.append(((x * Y + y) * CORES + core, (to_x % X * Y + to_y) * CORES + to_core))
    return pairs


TO_CORE = node_pairs(lambda x, y, core: (x, y, 1 - core))
TO_Y = node_pairs(lambda x, y, core: (x, 1 - y, core))
TO_FIRST = node_pairs(lambda x, y, core: (x + 1 - 2 * (x % 2), y, core))
TO_FAR = node_pairs(lambda x, y, core: (x + 2, y, core))
TO_SECOND = node_pairs(lambda x, y, core: (x - 1 + 2 * (x % 2), y, core))


def send(array, pairs):
    return lax.ppermute(array, "intra", pairs)


def round_to_step(values):
    largest = jnp.maximum(jnp.max(jnp.abs(values), axis=-1, keepdims=True), LOWEST)
    gap = largest - largest * (1.0 - 2.0**-24)
    step = gap * 2.0**18
    half = gap * 2.0**17
    shift = gap * (1.5 * 2.0**41)
    nearest = (values + shift) - shift
    return nearest + jnp.where(values - nearest >= half, step, 0.0)


def ordered(hidden, me, along_y_first):
    rows = hidden.shape[1]
    place = lax.broadcasted_iota(jnp.int32, (rows, rows), 0)
    row = lax.broadcasted_iota(jnp.int32, (rows, rows), 1)
    core = place // 64
    if along_y_first:
        y, x = place // 32 % 2, place // 8 % 4
    else:
        x, y = place // 16 % 4, place // 8 % 2
    own_x = me // 4
    x = (own_x + x * (1 - 2 * (own_x % 2)) + X) % X
    y = (y + me // 2) % Y
    core = (core + me) % CORES
    source = ((x * Y + y) * CORES + core) * SHARE + place % SHARE
    chosen = jnp.where(row == source, 1.0, 0.0).astype(jnp.bfloat16)
    return lax.dot_general(
        chosen, hidden, (((1,), (1,)), ((), ())), preferred_element_type=jnp.float32
    ).astype(jnp.bfloat16)


def gradient_kernel(share, along_y_first, waits, streamed, me_ref, hidden_ref, upstream_ref, *refs):
    refs = refs[waits:]
    keep_ref, send_ref = refs[:2]
    rows = 2 * SHARE * len(share)
    width = len(share) * BLOCK

    def column(step, owner, block):
        start = ((step * 2 + owner) * LAYER + share[block]) * BLOCK
        return start if isinstance(start, int) else pl.multiple_of(start, BLOCK)

    def copies(step):
        found = []
        for owner in range(2):
            place, arrived = refs[2:]
            source = upstream_ref.at[:, pl.ds(column(step, owner, 0), width)]
            found.append(pltpu.make_async_copy(source, place.at[step, owner], arrived.at[step, owner]))
        return found

    if streamed:
        for step in range(STEPS):
            for copy in copies(step):
                copy.start()
    left = ordered(hidden_ref[...], me_ref[0], along_y_first)

    def one_step(step, carry):
        blocks = [(owner, block) for owner in range(2) for block in range(len(share))]
        for pair in range(len(share)):
            both = []
            for owner, block in blocks[2 * pair : 2 * pair + 2]:
                if streamed:
                    upstream = refs[2][step, owner, :, block * BLOCK : (block + 1) * BLOCK]
                else:
                    upstream = upstream_ref[:, pl.ds(column(step, owner, block), BLOCK)]
                grad = jnp.dot(left, upstream, preferred_element_type=jnp.float32)
                both.append(round_to_step(grad).reshape(16, SHARE, BLOCK))
            both = jnp.concatenate(both, axis=1).astype(jnp.bfloat16)
            start = step * rows + pair * 2 * SHARE
            at = pl.ds(start if isinstance(start, int) else pl.multiple_of(start, 2 * SHARE), 2 * SHARE)
            keep_ref[:, at, :] = both[:8]
            send_ref[:, at, :] = both[8:]
        return carry

    if streamed:
        for begin, end in WAITS:
            for step in range(begin, end):
                for copy in copies(step):
                    copy.wait()
            for step in range(begin, end):
                one_step(step, 0)
    else:
        lax.fori_loop(0, STEPS, one_step, 0, unroll=True)


def gradients(me, hidden, upstream, share, along_y_first, room, streamed, after=()):
    tokens = upstream.shape[0]
    out = jax.ShapeDtypeStruct((8, OWNERS * len(share) * SHARE, BLOCK), jnp.bfloat16)
    scratch = [
        pltpu.VMEM((STEPS, 2, tokens, len(share) * BLOCK), jnp.bfloat16),
        pltpu.SemaphoreType.DMA((STEPS, 2)),
    ]
    return pl.pallas_call(
        functools.partial(gradient_kernel, share, along_y_first, len(after), streamed),
        in_specs=[
            pl.BlockSpec(memory_space=pltpu.SMEM),
            pl.BlockSpec(memory_space=pltpu.VMEM),
            pl.BlockSpec(memory_space=pltpu.HBM if streamed else pltpu.VMEM),
        ]
        + [pl.BlockSpec(memory_space=pl.ANY)] * len(after),
        out_specs=[pl.BlockSpec(memory_space=pltpu.VMEM)] * 2,
        out_shape=[out, out],
        scratch_shapes=scratch if streamed else [],
        compiler_params=pltpu.CompilerParams(vmem_limit_bytes=room * 2**20),
        cost_estimate=SMALL,
    )(me, hidden, upstream, *after)


def tiled_call(kernel, steps, ins, outs, after=()):
    shapes = [jax.ShapeDtypeStruct(tuple(lead) + (rows, BLOCK), dtype) for lead, rows, dtype in outs]

    def view(ref, step):
        tile = ref.shape[-2] // steps
        rows = pl.ds(pl.multiple_of(step * tile, tile), tile)
        return ref.at[(slice(None),) * (len(ref.shape) - 2) + (rows, slice(None))]

    def whole(*refs):
        used = refs[: len(ins)] + refs[len(ins) + len(after) :]

        def one_step(step, carry):
            kernel(*[view(ref, step) for ref in used])
            return carry

        lax.fori_loop(0, steps, one_step, 0, unroll=True)

    return pl.pallas_call(
        whole if steps > 1 else lambda *refs: kernel(*refs[: len(ins)], *refs[len(ins) + len(after) :]),
        in_specs=[pl.BlockSpec(memory_space=pltpu.VMEM)] * len(ins)
        + [pl.BlockSpec(memory_space=pl.ANY)] * len(after),
        out_specs=[pl.BlockSpec(memory_space=pltpu.VMEM)] * len(shapes),
        out_shape=shapes,
        compiler_params=PARAMS,
        cost_estimate=SMALL,
    )(*ins, *after)


def up(ref, *index):
    return ref[index].astype(jnp.float32) if index else ref[...].astype(jnp.float32)


def pair_kernel(keep_ref, got_ref, stay_ref, go_ref):
    for part in range(4):
        stay_ref[part] = up(keep_ref, part) + up(got_ref, part)
        go_ref[part] = up(keep_ref, part + 4) + up(got_ref, part + 4)


def add_kernel(keep_ref, got_ref, own_ref, first_ref, second_ref, first_later_ref, second_later_ref):
    def total(x, half):
        return up(keep_ref, x, half) + up(got_ref, x, half)

    own_ref[0], own_ref[1] = total(0, 0), total(0, 1)
    first_ref[0], first_ref[1] = total(2, 0), total(1, 0)
    second_ref[0], second_ref[1] = total(2, 1), total(3, 1)
    first_later_ref[...] = total(1, 1)
    second_later_ref[...] = total(3, 0)


def add_once_kernel(
    keep_ref, got_ref, first_ref, second_ref, from_first_ref, from_second_ref, own_ref, to_first_ref, far_ref, to_second_ref
):
    ahead = first_ref.shape[0]
    to_first_ref[:ahead] = first_ref[...] + from_second_ref[0]
    to_second_ref[:ahead] = second_ref[...] + from_first_ref[0]
    own_ref[...] = up(keep_ref, 0) + up(got_ref, 0)
    to_first_ref[ahead:] = up(keep_ref, 1) + up(got_ref, 1)
    far_ref[...] = up(keep_ref, 2) + up(got_ref, 2)
    to_second_ref[ahead:] = up(keep_ref, 3) + up(got_ref, 3)


def fold_kernel(first_ref, second_ref, from_first_ref, from_second_ref, to_first_ref, to_second_ref):
    to_first_ref[...] = first_ref[...] + from_second_ref[0]
    to_second_ref[...] = second_ref[...] + from_first_ref[0]


def halves(own_ref, from_first_ref, from_second_ref, later_first_ref, later_second_ref):
    first = own_ref[0] + from_first_ref[1] + later_second_ref[...]
    second = own_ref[1] + from_second_ref[1] + later_first_ref[...]
    return first, second


def node_pairs_kernel(own_ref, from_first_ref, from_second_ref, later_first_ref, later_second_ref, stay_ref, go_ref):
    stay_ref[...], go_ref[...] = halves(own_ref, from_first_ref, from_second_ref, later_first_ref, later_second_ref)


def nodes_kernel(*refs):
    out_ref = refs[-1]
    own_a_ref, from_first_ref, from_second_ref, own_c_ref, first_ref, second_ref, far_ref, stay_ref, got_ref = refs[:-1]
    ahead = own_a_ref.shape[1]
    a = (
        own_a_ref[0] + from_first_ref[1] + second_ref[:ahead],
        own_a_ref[1] + from_second_ref[1] + first_ref[:ahead],
    )
    a = jnp.concatenate([round_to_step(half).astype(jnp.bfloat16) for half in a], axis=0)
    c = own_c_ref[...] + first_ref[ahead:] + far_ref[...] + second_ref[ahead:]
    b = stay_ref[...] + got_ref[...]
    parts = [a, round_to_step(c).astype(jnp.bfloat16), round_to_step(b).astype(jnp.bfloat16)]
    at = 0
    for part in parts:
        rows = part.shape[0] // OWNERS
        for owner in range(OWNERS):
            out_ref[owner, at : at + rows] = part[owner * rows : (owner + 1) * rows]
        at += rows


def final_kernel(pieces_ref, one_ref, two_ref):
    total = up(pieces_ref, 0)
    for source in range(1, OWNERS):
        total = total + up(pieces_ref, source)
    for block in range(LAYER):
        columns = slice(block * BLOCK, (block + 1) * BLOCK)
        one_ref[:, columns] = total[block * SHARE : (block + 1) * SHARE]
        two_ref[:, columns] = total[(LAYER + block) * SHARE : (LAYER + block + 1) * SHARE]


def start_x(keep, got, after=()):
    rows = keep.shape[2]
    f32 = jnp.float32
    own, first, second, first_later, second_later = tiled_call(
        add_kernel, 4, (keep, got), [((2,), rows, f32)] * 3 + [((), rows, f32)] * 2, after
    )
    return own, first_later, second_later, send(first, TO_FIRST), send(second, TO_SECOND)


def end_x(own, first_later, second_later, from_first, from_second, after=()):
    rows = own.shape[1]
    first, second = tiled_call(
        fold_kernel, 1, (first_later, second_later, from_first, from_second), [((), rows, jnp.float32)] * 2, after
    )
    return (own, from_first, from_second, send(first, TO_FIRST), send(second, TO_SECOND)), (first, second)


def body(hidden_one, upstream_one, hidden_two, upstream_two):
    f32, bf16 = jnp.float32, jnp.bfloat16
    me = lax.axis_index("intra").astype(jnp.int32).reshape(1)

    def pair(keep, got, after=()):
        return tiled_call(pair_kernel, 4, (keep, got), [((4,), keep.shape[1], f32)] * 2, after)

    def halved(array, parts):
        rows = array.size // BLOCK // parts // 2
        return array.reshape(parts, 2, rows, BLOCK)

    keep_b, go_b = gradients(me, hidden_two, upstream_two, tuple(range(LAYER)), False, ROOM[0], True)
    core_b = send(go_b, TO_CORE)
    keep_a, go_a = gradients(me, hidden_one, upstream_one, tuple(range(FIRST)), True, ROOM[1], False)
    core_a = send(go_a, TO_CORE)
    b = start_x(halved(keep_b, 4), halved(core_b, 4))
    stay_a, go_a = pair(keep_a, core_a, (b[0],))
    y_a = send(go_a, TO_Y)
    keep_c, go_c = gradients(me, hidden_one, upstream_one, tuple(range(FIRST, LAYER)), True, ROOM[2], False, (stay_a,))
    core_c = send(go_c, TO_CORE)
    stay_c, go_c = pair(keep_c, core_c)
    y_c = send(go_c, TO_Y)

    b, sent_b = end_x(*b, (go_c,))
    a = start_x(halved(stay_a, 4), halved(y_a, 4), sent_b)
    stay_b, go_b = tiled_call(node_pairs_kernel, 2, b, [((), b[0].shape[1], f32)] * 2, (a[0],))
    y_b = send(go_b, TO_Y)
    rows, ahead = stay_c.shape[1], a[1].shape[0]
    own_c, first, far, second = tiled_call(
        add_once_kernel,
        1,
        (stay_c, y_c, *a[1:]),
        [((), rows, f32), ((), ahead + rows, f32), ((), rows, f32), ((), ahead + rows, f32)],
        (go_b,),
    )
    first, second, far = send(first, TO_FIRST), send(second, TO_SECOND), send(far, TO_FAR)

    node = pl.pallas_call(
        nodes_kernel,
        in_specs=[pl.BlockSpec(memory_space=pltpu.VMEM)] * 9,
        out_specs=pl.BlockSpec(memory_space=pltpu.VMEM),
        out_shape=jax.ShapeDtypeStruct((OWNERS, 2 * LAYER * SHARE, BLOCK), bf16),
        compiler_params=PARAMS,
        cost_estimate=SMALL,
    )(a[0], a[3], a[4], own_c, first, second, far, stay_b, y_b)
    pieces = lax.all_to_all(node, "inter", split_axis=0, concat_axis=0, tiled=True)
    out = jax.ShapeDtypeStruct((SHARE, LAYER * BLOCK), f32)
    vmem = pl.BlockSpec(memory_space=pltpu.VMEM)
    return pl.pallas_call(final_kernel, in_specs=[vmem], out_shape=(out, out))(pieces)


def solution(mesh):
    return jax.shard_map(
        body,
        mesh=mesh,
        in_specs=(
            P(("intra", "inter"), None),
            P(("intra", "inter"), None),
            P(("intra", "inter"), None),
            P(("intra", "inter"), None),
        ),
        out_specs=(P("intra", "inter"), P("intra", "inter")),
        check_vma=False,
    )
```
